1024 devices in a mesh: dp: 64 (over z, core), expert: 16 (over y, x).
Axes of the slice: x: 4, y: 4, z: 32, core: 2. Of those that a mesh axis runs over, the one named last changes fastest.
Arguments:
- tokens: bfloat16 [512, 3072], P('dp', 'expert'), may hold values from -6 to 6
- grad_out: bfloat16 [512, 3072], P('dp', 'expert'), may hold values from -1.5 to 1.5
- routes: int32 [512, 4], P('dp'), may hold values from 0 to 15, all different within a row; in each aligned block of 8 rows (0 to 7, 8 to 15, ...) at most 4 rows name the same one
- gate_probs: float32 [512, 4], P('dp'), may hold values from 0.1 to 1
- w_gate: bfloat16 [16, 6144, 3072], P('expert', 'dp'), may hold values from -0.109375 to 0.109375
- w_up: bfloat16 [16, 6144, 3072], P('expert', 'dp'), may hold values from -0.109375 to 0.109375
- w_down: bfloat16 [16, 6144, 3072], P('expert', 'dp'), may hold values from -0.078125 to 0.078125
Outputs:
- grad_in: bfloat16 [512, 3072], P('dp', 'expert')
- grad_gate: bfloat16 [16, 6144, 3072], P('expert', 'dp')
- grad_up: bfloat16 [16, 6144, 3072], P('expert', 'dp')
- grad_down: bfloat16 [16, 6144, 3072], P('expert', 'dp')
The draws below stay inside these ranges and needn't reach their ends.
Inputs may be any that keep to these rules, and one draw needn't show every extreme that they name: `routes`: each token names 4 different experts. Among the 8 tokens of one dp index no expert is named more than 4 times, and in every draw some expert is named exactly 4 times by the tokens of some dp index.
All inputs are finite; a program needn't handle non-finite values.
Results may differ from the reference program's by a relative error of at most 0.0064.
Values may be sent and summed in bfloat16 or wider, within the bound.
No kernel may reach another device: no remote copies, remote signals or barrier semaphores. Data moves between devices by JAX's collectives and lax.ppermute only.
A program may use at most 32 MiB of HBM per device.

```python
import math
from functools import partial
import jax
import jax.numpy as jnp
import numpy as np
from jax import lax

D = 3072
FF = 6144
EXPERTS = 16
TOP = 4
CAP = 4
TOK_ROW = 8
TOKENS = 512


def block_levels(stream_key, extent, split, low, largest):
    factor_of = 1.0
    for position, blocks in split:
        heights = jax.random.uniform(jax.random.fold_in(jax.random.fold_in(stream_key, 6), position), (blocks,), jnp.float32, low / len(split), largest / len(split))
        factor_of = factor_of * jnp.repeat(jnp.exp(heights), extent[position] // blocks).reshape((-1,) + (1,) * (len(extent) - 1 - position))
    return factor_of


def shared_out(rng, own, number, rows, count, top, limit, lean):
    sequence = jax.random.permutation(rng, count)
    heavy_load, usual = portions_of(count, rows * top, limit, lean, True), portions_of(count, rows * top, limit, lean, False)
    places = jnp.arange(count)

    def named(lengths, offset_by):
        used = int((lengths > 0).sum())
        fixed = max(1, used // 4)
        moved = fixed + (places - fixed + offset_by * (used - fixed)) % max(1, count - fixed)
        return jnp.zeros((count,), jnp.int32).at[sequence[jnp.where(places < fixed, places, moved)]].set(jnp.asarray(lengths, jnp.int32))

    lengths = jnp.where(number % 4 == 0, named(heavy_load, number // 4), named(usual, number - number // 4 - 1))
    mixed = jax.random.permutation(jax.random.fold_in(own, 3), count)
    giver, sink = mixed[0:count // 2 * 2:2], mixed[1:count // 2 * 2:2]
    slack = jnp.minimum(lengths[giver] - 1, limit - lengths[sink]) // 2
    slack = jnp.where((giver == sequence[0]) | (sink == sequence[0]) | (lengths[sink] == 0), 0, jnp.maximum(slack, 0))
    moved = jax.random.randint(jax.random.fold_in(own, 4), (count // 2,), 0, 1 << 20) % (slack + 1)
    lengths = lengths.at[giver].add(-moved).at[sink].add(moved)
    labels = jnp.searchsorted(jnp.cumsum(lengths), jnp.arange(rows * top), side="right").astype(jnp.int32)
    table = labels.reshape(top, rows).T
    table = table[jax.random.permutation(jax.random.fold_in(own, 1), rows)]
    offset_by = jax.random.randint(jax.random.fold_in(own, 2), (rows, 1), 0, top)
    return jnp.take_along_axis(table, (jnp.arange(top)[None, :] + offset_by) % top, axis=1)


def portions_of(amount, total, limit, lean, full):
    portions = [(1 << 20) // math.isqrt(rank ** lean) + 1 for rank in range(1, amount + 1)]
    largest = limit if full else min(limit, max(-(-total // amount), total * portions[0] // sum(portions)))
    least = 1 if total - largest >= amount - 1 else 0
    holding, spare = [largest] + [least] * (amount - 1), total - largest - least * (amount - 1)
    while spare > 0:
        free = [i for i in range(1, amount) if holding[i] < largest] or [i for i in range(1, amount) if holding[i] < limit]
        mass, remaining = sum([portions[i] for i in free]), spare
        for i in free:
            more = min(limit - holding[i], max(1, remaining * portions[i] // mass), spare)
            holding[i] = holding[i] + more
            spare = spare - more
    return np.array(holding)


def scatter_about(key, dims, width, bound, split=(), kind=jnp.bfloat16):
    drawn = jax.random.normal(key, dims, jnp.float32) * width
    if len(split) > 0:
        drawn = block_levels(key, dims, split, -0.22, 0.18) * drawn
    return jnp.clip(drawn, min=-bound, max=bound).astype(kind)


def setup_inputs(seed: int = 0) -> dict:
    keys = jax.random.split(jax.random.key(seed), 8)
    tokens = scatter_about(keys[0], (TOKENS, D), 1.0, 6.0, ((0, 64), (1, 16)))
    grad_out = scatter_about(keys[1], (TOKENS, D), 0.25, 1.5, ((0, 64), (1, 16)))
    routes_keys = jax.random.split(jax.random.fold_in(keys[2], 1), TOKENS // TOK_ROW)
    routes_turns = jax.random.permutation(jax.random.fold_in(keys[2], 3), TOKENS // TOK_ROW)
    routes = jax.vmap(lambda own, number: shared_out(jax.random.fold_in(keys[2], 2), own, number, TOK_ROW, EXPERTS, TOP, CAP, 2))(routes_keys, routes_turns).reshape((TOKENS, TOP))
    gate_probs = jnp.clip(jnp.exp(math.log(1.0) - 2.3025851 * jax.random.uniform(keys[3], (TOKENS, TOP), jnp.float32) ** block_levels(keys[3], (TOKENS, TOP), ((0, 64),), -0.2, 0.2)), 0.1, 1.0)
    w_gate = scatter_about(keys[4], (EXPERTS, FF, D), D ** -0.5, 0.109375, ((0, 16), (1, 64)))
    w_up = scatter_about(keys[5], (EXPERTS, FF, D), D ** -0.5, 0.109375, ((0, 16), (1, 64)))
    w_down = scatter_about(keys[6], (EXPERTS, FF, D), FF ** -0.5, 0.078125, ((0, 16), (1, 64)))
    return dict(tokens=tokens, grad_out=grad_out, routes=routes, gate_probs=gate_probs, w_gate=w_gate, w_up=w_up, w_down=w_down)


def silu_parts(pre_act):
    sigmoid_val = jax.nn.sigmoid(pre_act)
    return pre_act * sigmoid_val, sigmoid_val * (1.0 + pre_act * (1.0 - sigmoid_val))


def slot_tables(route_rows, prob_rows, experts, capacity):
    tok_rows, top_k = route_rows.shape
    flat_routes = route_rows.reshape(tok_rows * top_k).astype(jnp.int32)
    onehot = (flat_routes[:, None] == jnp.arange(experts, dtype=jnp.int32)[None, :]).astype(jnp.int32)
    before = jnp.cumsum(onehot, axis=0) - onehot
    slot_index = jnp.sum(onehot * before, axis=1)
    slot_place = slot_index * experts + flat_routes
    placement = (slot_place[:, None] == jnp.arange(capacity * experts, dtype=jnp.int32)[None, :]).astype(prob_rows.dtype)
    placement = placement.reshape(tok_rows, top_k, capacity * experts)
    dispatch = jnp.sum(placement, axis=1)
    weighted = jnp.sum(placement * prob_rows[:, :, None], axis=1)
    return dispatch, weighted


def expert_grads(expert_item):
    rows_in, rows_grad, gate_mat, up_mat, down_mat = expert_item
    inner = (((1,), (1,)), ((), ()))
    pre_act = lax.dot_general(rows_in, gate_mat, inner, preferred_element_type=jnp.float32)
    up_value = lax.dot_general(rows_in, up_mat, inner, preferred_element_type=jnp.float32)
    silu_val, silu_slope = silu_parts(pre_act)
    activation = (silu_val * up_value).astype(jnp.bfloat16)
    grad_act = lax.dot_general(rows_grad, down_mat, inner, preferred_element_type=jnp.float32)
    grad_pre = (grad_act * up_value * silu_slope).astype(jnp.bfloat16)
    grad_upv = (grad_act * silu_val).astype(jnp.bfloat16)
    rows_first = (((0,), (0,)), ((), ()))
    grad_gate = lax.dot_general(grad_pre, rows_in, rows_first, preferred_element_type=jnp.float32).astype(jnp.bfloat16)
    grad_up = lax.dot_general(grad_upv, rows_in, rows_first, preferred_element_type=jnp.float32).astype(jnp.bfloat16)
    grad_down = lax.dot_general(activation, rows_grad, rows_first, preferred_element_type=jnp.float32).astype(jnp.bfloat16)
    back_rows = jnp.dot(grad_pre, gate_mat, preferred_element_type=jnp.float32)
    back_rows = back_rows + jnp.dot(grad_upv, up_mat, preferred_element_type=jnp.float32)
    return grad_gate, grad_up, grad_down, back_rows.astype(jnp.bfloat16)


def reference(tokens, grad_out, routes, gate_probs, w_gate, w_up, w_down):
    groups = TOKENS // TOK_ROW
    slots = CAP * EXPERTS
    tables = jax.vmap(partial(slot_tables, experts=EXPERTS, capacity=CAP))
    dispatch, weighted = tables(routes.reshape(groups, TOK_ROW, TOP), gate_probs.reshape(groups, TOK_ROW, TOP))
    token_rows = tokens.reshape(groups, TOK_ROW, D).astype(jnp.float32)
    cotangent = grad_out.reshape(groups, TOK_ROW, D).astype(jnp.float32)
    highest = lax.Precision.HIGHEST
    packed_in = jnp.einsum("gts,gtf->gsf", dispatch, token_rows, precision=highest).astype(jnp.bfloat16)
    packed_grad = jnp.einsum("gts,gtf->gsf", weighted, cotangent, precision=highest).astype(jnp.bfloat16)

    def by_expert(packed):
        return packed.reshape(groups, CAP, EXPERTS, D).transpose(2, 0, 1, 3).reshape(EXPERTS, groups * CAP, D)

    grad_gate, grad_up, grad_down, back_rows = lax.map(
        expert_grads, (by_expert(packed_in), by_expert(packed_grad), w_gate, w_up, w_down))
    back_rows = back_rows.reshape(EXPERTS, groups, CAP, D).transpose(1, 2, 0, 3).reshape(groups, slots, D)
    grad_in = jnp.einsum("gts,gsf->gtf", dispatch, back_rows.astype(jnp.float32), precision=highest)
    grad_in = grad_in.astype(jnp.bfloat16).reshape(TOKENS, D)
    return grad_in, grad_gate, grad_up, grad_down
```

```python
import jax
import jax.numpy as jnp
from jax import lax
from jax.experimental import pallas as pl
from jax.experimental.pallas import tpu as pltpu
from jax.sharding import Mesh, PartitionSpec as P

EXPERTS = 16
CAP = 4
TOP = 4
FAR = 8
NEAR = 4
BF16 = jnp.bfloat16
F32 = jnp.float32
VMEM_BYTES = 48 * 1024 * 1024
GRAD_AT = 256
ROW = 512


def message_kernel(tokens_ref, grad_ref, routes_ref, probs_ref, out_ref):
    tok_rows, width = tokens_ref.shape
    routes = routes_ref[...].astype(F32)
    probs = probs_ref[...]
    lane = lax.broadcasted_iota(jnp.int32, (tok_rows, 128), 1)
    row = lax.broadcasted_iota(jnp.int32, (tok_rows, 128), 0)
    lane_f = lane.astype(F32)
    onehot = jnp.zeros((tok_rows, 128), F32)
    for k in range(TOP):
        onehot = jnp.where(lane_f == routes[:, k : k + 1], 1.0, onehot)
    before = jnp.zeros((tok_rows, 128), F32)
    for s in range(1, tok_rows):
        before = before + jnp.where(row >= s, pltpu.roll(onehot, s, 0), 0.0)
    meta = jnp.zeros((tok_rows, 128), F32)
    base = width - 128
    for k in range(TOP):
        chosen = routes[:, k : k + 1]
        slot = jnp.sum(jnp.where(lane_f == chosen, before, 0.0), axis=1, keepdims=True)
        meta = jnp.where(lane == base + k, chosen * CAP + slot, meta)
        rest = probs[:, k : k + 1]
        for part in range(3):
            piece = rest.astype(BF16).astype(F32)
            meta = jnp.where(lane == base + (part + 1) * TOP + k, piece, meta)
            rest = rest - piece
    meta = meta.astype(BF16)
    tail = jnp.zeros((tok_rows, 128), BF16)
    for copy in range(out_ref.shape[0]):
        out_ref[copy, :, 128:256] = meta
        out_ref[copy, :, 0:width] = tokens_ref[...]
        out_ref[copy, :, GRAD_AT + 128 : GRAD_AT + 256] = tail
        out_ref[copy, :, GRAD_AT : GRAD_AT + width] = grad_ref[...]


def message(tokens, grad_out, routes, probs):
    return pl.pallas_call(
        message_kernel,
        out_shape=jax.ShapeDtypeStruct((FAR, tokens.shape[0], ROW), BF16),
    )(tokens, grad_out, routes, probs)


def pack_kernel(msg_ref, out_ref, place_ref, diff_ref):
    toks = msg_ref.shape[0]
    width = out_ref.shape[1]
    rows = out_ref.shape[2] // 2
    left = msg_ref[:, 0:256].astype(F32)
    feats = jnp.transpose(left).astype(BF16)[:width]
    cots = jnp.transpose(msg_ref[:, GRAD_AT : GRAD_AT + 256].astype(F32)).astype(BF16)[:width]
    tok = lax.broadcasted_iota(jnp.int32, (toks, rows), 0)
    row = lax.broadcasted_iota(jnp.int32, (toks, rows), 1)
    same = (tok >> 3) == (row >> 2)
    slot = (row & 3).astype(F32)
    weights = []
    for k in range(TOP):
        code = left[:, width + k : width + k + 1]
        diff_ref[k] = jnp.where(same, code - slot, -1.0)
        at = width + TOP + k
        weights.append(
            left[:, at : at + 1] + left[:, at + TOP : at + TOP + 1]
            + left[:, at + 2 * TOP : at + 2 * TOP + 1]
        )

    @pl.loop(0, EXPERTS)
    def _(e):
        wanted = (e * CAP).astype(F32)
        here = jnp.zeros((toks, rows), F32)
        weight = jnp.zeros((toks, rows), F32)
        for k in range(TOP):
            hit = diff_ref[k] == wanted
            here = jnp.where(hit, 1.0, here)
            weight = jnp.where(hit, weights[k], weight)
        place = here.astype(BF16)
        scale = jnp.sum(weight, axis=0, keepdims=True)
        place_ref[e] = place
        out_ref[e, :, 0:rows] = jnp.dot(feats, place, preferred_element_type=F32).astype(BF16)
        out_ref[e, :, rows:] = (
            jnp.dot(cots, place, preferred_element_type=F32) * scale
        ).astype(BF16)


def pack(msgs, width):
    toks = msgs.shape[0]
    rows = toks // 2
    return pl.pallas_call(
        pack_kernel,
        out_shape=(
            jax.ShapeDtypeStruct((EXPERTS, width, 2 * rows), BF16),
            jax.ShapeDtypeStruct((EXPERTS, toks, rows), BF16),
        ),
        scratch_shapes=[pltpu.VMEM((TOP, toks, rows), F32)],
        compiler_params=pltpu.CompilerParams(vmem_limit_bytes=VMEM_BYTES),
    )(msgs)


LAST = (((1,), (1,)), ((), ()))
FIRST = (((0,), (0,)), ((), ()))
STEP = 512


def expert_kernel(
    own_ref, oth_ref, wg_ref, wu_ref, wd_ref, gg_ref, gu_ref, gd_ref, keep_ref, send_ref
):
    dim, both = own_ref.shape
    half = both // 2
    units = wg_ref.shape[0]

    def rows_in(at):
        return jnp.concatenate([own_ref[at, :half], oth_ref[at, :half]], axis=1)

    def rows_grad(at):
        return jnp.concatenate([own_ref[at, half:], oth_ref[at, half:]], axis=1)

    def two(at):
        return jnp.concatenate([wg_ref[:, at], wu_ref[:, at]], axis=0)

    fwd = jnp.zeros((2 * units, both), F32)
    grad_act = jnp.zeros((units, both), F32)
    for i in range(dim // STEP):
        at = pl.ds(i * STEP, STEP)
        fwd = fwd + jnp.dot(two(at), rows_in(at), preferred_element_type=F32)
        grad_act = grad_act + jnp.dot(wd_ref[:, at], rows_grad(at), preferred_element_type=F32)
    pre_act, up_value = fwd[:units], fwd[units:]
    sig = jax.nn.sigmoid(pre_act)
    silu = pre_act * sig
    slope = sig * (1.0 + pre_act * (1.0 - sig))
    activation = (silu * up_value).astype(BF16)
    grad_pre = (grad_act * up_value * slope).astype(BF16)
    grad_upv = (grad_act * silu).astype(BF16)
    cots = jnp.concatenate([grad_pre, grad_upv], axis=0)
    for i in range(dim // STEP):
        at = pl.ds(i * STEP, STEP)
        total = lax.dot_general(two(at), cots, FIRST, preferred_element_type=F32)
        keep_ref[at, :] = total[:, :half]
        send_ref[at, :] = total[:, half:].astype(BF16)
        grads = lax.dot_general(cots, rows_in(at), LAST, preferred_element_type=F32).astype(BF16)
        gg_ref[:, at] = grads[:units]
        gu_ref[:, at] = grads[units:]
        gd_ref[:, at] = lax.dot_general(
            activation, rows_grad(at), LAST, preferred_element_type=F32
        ).astype(BF16)


def expert(own, oth, w_gate, w_up, w_down):
    dim, both = own.shape
    grad = jax.ShapeDtypeStruct(w_gate.shape, BF16)
    return pl.pallas_call(
        expert_kernel,
        out_shape=(
            grad,
            grad,
            grad,
            jax.ShapeDtypeStruct((dim, both // 2), F32),
            jax.ShapeDtypeStruct((dim, both // 2), BF16),
        ),
        compiler_params=pltpu.CompilerParams(vmem_limit_bytes=VMEM_BYTES),
    )(own, oth, w_gate, w_up, w_down)


def combine_kernel(back_ref, place_ref, out_ref):
    width, toks = back_ref.shape[1], place_ref.shape[1]

    def add(e, total):
        return total + lax.dot_general(
            back_ref[e], place_ref[e], LAST, preferred_element_type=F32
        )

    total = lax.fori_loop(0, EXPERTS, add, jnp.zeros((width, toks), F32))
    out_ref[...] = jnp.transpose(total)


def combine(back, place):
    return pl.pallas_call(
        combine_kernel,
        out_shape=jax.ShapeDtypeStruct((place.shape[1], back.shape[1]), F32),
        compiler_params=pltpu.CompilerParams(vmem_limit_bytes=VMEM_BYTES),
    )(back, place)


def exchange(value, axis):
    return lax.all_to_all(value, axis, split_axis=0, concat_axis=0, tiled=True)


SWAP = [(0, 1), (1, 0)]


def shards(tokens, grad_out, routes, gate_probs, w_gate, w_up, w_down):
    tok_rows, width = tokens.shape
    dim = w_gate.shape[2]
    w_gate, w_up, w_down = w_gate[0], w_up[0], w_down[0]
    far = exchange(message(tokens, grad_out, routes, gate_probs), "far")
    far = far.reshape(1, FAR * tok_rows, ROW)
    near = exchange(jnp.broadcast_to(far, (NEAR, FAR * tok_rows, ROW)), "near")
    slots, place = pack(near.reshape(NEAR * FAR * tok_rows, ROW), width)
    own = exchange(slots, ("y", "x")).reshape(dim, -1)
    oth = lax.ppermute(own, "core", SWAP)
    grad_gate, grad_up, grad_down, keep, send = expert(own, oth, w_gate, w_up, w_down)
    back = (keep + lax.ppermute(send, "core", SWAP).astype(F32)).astype(BF16)
    back = exchange(back.reshape(EXPERTS, width, -1), ("y", "x"))
    part = combine(back, place)
    part = exchange(part.reshape(NEAR, FAR * tok_rows, width), "near").sum(axis=0)
    part = exchange(part.reshape(FAR, tok_rows, width), "far").sum(axis=0)
    return part.astype(BF16), grad_gate[None], grad_up[None], grad_down[None]


def solution(mesh):
    fine = Mesh(
        mesh.devices.reshape(FAR, NEAR, 2, 4, 4), ("far", "near", "core", "y", "x")
    )
    dp, expert_axes = ("far", "near", "core"), ("y", "x")
    in_specs = (
        P(dp, expert_axes),
        P(dp, expert_axes),
        P(dp, None),
        P(dp, None),
        P(expert_axes, dp, None),
        P(expert_axes, dp, None),
        P(expert_axes, dp, None),
    )
    out_specs = (
        P(dp, expert_axes),
        P(expert_axes, dp, None),
        P(expert_axes, dp, None),
        P(expert_axes, dp, None),
    )
    return jax.shard_map(shards, mesh=fine, in_specs=in_specs, out_specs=out_specs, check_vma=False)
```

```python
import jax
import jax.numpy as jnp
from jax import lax
from jax.experimental import pallas as pl
from jax.experimental.pallas import tpu as pltpu
from jax.sharding import Mesh, PartitionSpec as P

EXPERTS = 16
CAP = 4
TOP = 4
FAR = 16
PAIR = 2
BF16 = jnp.bfloat16
F32 = jnp.float32
VMEM_BYTES = 24 * 1024 * 1024
LAST = (((1,), (1,)), ((), ()))
FIRST = (((0,), (0,)), ((), ()))
GRAD_AT = 256
ROW = 512
STEP = 384


def iota(shape, dim):
    return lax.broadcasted_iota(jnp.int32, shape, dim)


def message_kernel(tokens_ref, grad_ref, routes_ref, probs_ref, out_ref):
    tok_rows, width = tokens_ref.shape
    eye = iota((tok_rows, tok_rows), 0) == iota((tok_rows, tok_rows), 1)

    def column(values):
        spread = jnp.broadcast_to(values, (tok_rows, tok_rows))
        return jnp.sum(jnp.where(eye, spread, 0.0), axis=1, keepdims=True)

    lane = iota((tok_rows, 128), 1)
    row = iota((tok_rows, 128), 0)
    expert_at = (lane & (EXPERTS - 1)).astype(F32)
    chosen = jnp.zeros((tok_rows, 128), F32)
    weight = jnp.zeros((tok_rows, 128), F32)
    for k in range(TOP):
        hit = expert_at == column(routes_ref[k : k + 1, :].astype(F32))
        chosen = jnp.where(hit, 1.0, chosen)
        weight = jnp.where(hit, column(probs_ref[k : k + 1, :]), weight)
    before = jnp.zeros((tok_rows, 128), F32)
    for s in range(1, tok_rows):
        before = before + jnp.where(row >= s, pltpu.roll(chosen, s, 0), 0.0)
    kind = lane >> 4
    meta = jnp.where(kind == 4, jnp.where(chosen > 0.0, before, -1.0), 0.0)
    rest = weight
    for part in range(3):
        piece = rest.astype(BF16).astype(F32)
        meta = jnp.where(kind == 5 + part, piece, meta)
        rest = rest - piece
    meta = meta.astype(BF16)
    blank = jnp.zeros((tok_rows, 128), BF16)
    for copy in range(out_ref.shape[0]):
        out_ref[copy, :, 128:256] = meta
        out_ref[copy, :, 0:width] = tokens_ref[...]
        out_ref[copy, :, GRAD_AT + 128 : ROW] = blank
        out_ref[copy, :, GRAD_AT : GRAD_AT + width] = grad_ref[...]


def message(tokens, grad_out, routes, probs):
    return pl.pallas_call(
        message_kernel,
        out_shape=jax.ShapeDtypeStruct((FAR, tokens.shape[0], ROW), BF16),
    )(tokens, grad_out, routes.T, probs.T)


def pack_kernel(pair_ref, msg_ref, out_ref, table_ref):
    toks = msg_ref.shape[0]
    width, lanes = out_ref.shape[1:]
    half = lanes // 2
    left = msg_ref[:, 0:GRAD_AT].astype(F32)
    left_t = jnp.transpose(left)
    right_t = jnp.transpose(msg_ref[:, GRAD_AT:ROW].astype(F32))
    table_ref[...] = left_t[width : width + EXPERTS]
    top = jnp.concatenate([left_t[:width], right_t[:width]], axis=1)
    parts = left_t[width + EXPERTS : width + 4 * EXPERTS]
    low = jnp.concatenate([jnp.zeros_like(parts), parts], axis=1)
    lhs = jnp.concatenate([top, low], axis=0).astype(BF16)
    pair = pair_ref[0]
    tok = iota((2 * toks, lanes), 0)
    lane = iota((2 * toks, lanes), 1)
    row = lane & (half - 1)
    is_in = (lane >= half) == (pair == 1)
    fits = (((tok & (toks - 1)) >> 3) == (row >> 2)) & ((tok < toks) == is_in)
    wanted = jnp.where(fits, (row & 3).astype(F32), 9.0)
    in_lane = (iota((1, lanes), 1) >= half) == (pair == 1)
    for e in range(0, EXPERTS, 2):
        places = []
        for j in (e, e + 1):
            slot = left[:, width + j : width + j + 1]
            slot = jnp.concatenate([slot, slot], axis=0)
            places.append(jnp.where(slot == wanted, 1.0, 0.0))
        place = jnp.concatenate(places, axis=1).astype(BF16)
        both = jnp.dot(lhs, place, preferred_element_type=F32)
        for j in (0, 1):
            block = both[:, j * lanes : (j + 1) * lanes]
            scale = block[width + e + j : width + e + j + 1]
            for part in (1, 2):
                at = width + part * EXPERTS + e + j
                scale = scale + block[at : at + 1]
            scale = jnp.where(in_lane, 1.0, scale)
            packed = (block[:width] * scale).astype(BF16)
            for p in range(PAIR):
                out_ref[p * EXPERTS + e + j] = packed


def pack(pair, msgs, width):
    toks = msgs.shape[0]
    return pl.pallas_call(
        pack_kernel,
        in_specs=[
            pl.BlockSpec(memory_space=pltpu.SMEM),
            pl.BlockSpec(memory_space=pltpu.VMEM),
        ],
        out_shape=(
            jax.ShapeDtypeStruct((PAIR * EXPERTS, width, toks), BF16),
            jax.ShapeDtypeStruct((EXPERTS, toks), F32),
        ),
        compiler_params=pltpu.CompilerParams(vmem_limit_bytes=VMEM_BYTES),
    )(pair, msgs)


def rows_at(own_ref, oth_ref, at):
    lanes = own_ref.shape[2]
    first = iota((at.size, lanes), 1) < lanes // 2
    ins, cots = [], []
    for ref in (own_ref, oth_ref):
        even, odd = ref[0, at, :], ref[1, at, :]
        ins.append(jnp.where(first, even, odd))
        cots.append(jnp.where(first, odd, even))
    return jnp.concatenate(ins, axis=1), jnp.concatenate(cots, axis=1)


def turn(value, lanes):
    blocks = [
        pltpu.roll(value[:, at : at + lanes], lanes // 2, 1)
        for at in range(0, value.shape[1], lanes)
    ]
    return jnp.concatenate(blocks, axis=1)


def expert_kernel(
    own_ref, oth_ref, wg_ref, wu_ref, wd_ref, keep_ref, send_ref, cots_ref, act_ref
):
    dim, lanes = own_ref.shape[1:]
    units = wg_ref.shape[0]
    width = keep_ref.shape[2] * 2

    def two(at):
        return jnp.concatenate([wg_ref[:, at], wu_ref[:, at]], axis=0)

    fwd = jnp.zeros((2 * units, 2 * lanes), F32)
    grad_act = jnp.zeros((units, 2 * lanes), F32)
    for i in range(dim // STEP):
        at = pl.ds(i * STEP, STEP)
        rows_in, rows_grad = rows_at(own_ref, oth_ref, at)
        fwd = fwd + jnp.dot(two(at), rows_in, preferred_element_type=F32)
        grad_act = grad_act + jnp.dot(wd_ref[:, at], rows_grad, preferred_element_type=F32)
    grad_act = turn(grad_act, lanes)
    pre_act, up_value = fwd[:units], fwd[units:]
    sig = jax.nn.sigmoid(pre_act)
    silu = pre_act * sig
    slope = sig * (1.0 + pre_act * (1.0 - sig))
    act_ref[...] = turn(silu * up_value, lanes).astype(BF16)
    grad_pre = (grad_act * up_value * slope).astype(BF16)
    grad_upv = (grad_act * silu).astype(BF16)
    cots = jnp.concatenate([grad_pre, grad_upv], axis=0)
    cots_ref[...] = cots
    first = iota((width // 2, lanes), 1) < lanes // 2
    for i in range(dim // STEP):
        at = pl.ds(i * STEP, STEP)
        total = lax.dot_general(two(at), cots, FIRST, preferred_element_type=F32)
        for j in range(STEP // width):
            e = i * (STEP // width) + j
            for ref, begin in ((keep_ref, 0), (send_ref, lanes)):
                block = total[j * width : (j + 1) * width, begin : begin + lanes]
                upper, lower = block[: width // 2], block[width // 2 :]
                even = jnp.where(first, upper, pltpu.roll(lower, lanes // 2, 1))
                odd = jnp.where(first, pltpu.roll(upper, lanes // 2, 1), lower)
                ref[0, e] = even.astype(ref.dtype)
                ref[1, e] = odd.astype(ref.dtype)


def expert(own, oth, w_gate, w_up, w_down, width):
    units, dim = w_gate.shape
    lanes = own.shape[2]
    back = (PAIR, EXPERTS, width // 2, lanes)
    return pl.pallas_call(
        expert_kernel,
        out_shape=(
            jax.ShapeDtypeStruct(back, F32),
            jax.ShapeDtypeStruct(back, BF16),
            jax.ShapeDtypeStruct((2 * units, 2 * lanes), BF16),
            jax.ShapeDtypeStruct((units, 2 * lanes), BF16),
        ),
        cost_estimate=pl.CostEstimate(
            flops=2 * 5 * units * dim * 2 * lanes, bytes_accessed=9 << 20, transcendentals=0
        ),
        compiler_params=pltpu.CompilerParams(vmem_limit_bytes=VMEM_BYTES),
    )(own, oth, w_gate, w_up, w_down)


def grads_kernel(own_ref, oth_ref, cots_ref, act_ref, gg_ref, gu_ref, gd_ref):
    units, dim = gg_ref.shape
    for i in range(dim // STEP):
        at = pl.ds(i * STEP, STEP)
        rows_in, rows_grad = rows_at(own_ref, oth_ref, at)
        grads = lax.dot_general(cots_ref[...], rows_in, LAST, preferred_element_type=F32)
        grads = grads.astype(BF16)
        gg_ref[:, at] = grads[:units]
        gu_ref[:, at] = grads[units:]
        gd_ref[:, at] = lax.dot_general(
            act_ref[...], rows_grad, LAST, preferred_element_type=F32
        ).astype(BF16)


def weight_grads(own, oth, cots, act):
    units, dim = act.shape[0], own.shape[1]
    grad = jax.ShapeDtypeStruct((units, dim), BF16)
    return pl.pallas_call(
        grads_kernel,
        out_shape=(grad, grad, grad),
        cost_estimate=pl.CostEstimate(
            flops=2 * 3 * units * dim * act.shape[1], bytes_accessed=5 << 20, transcendentals=0
        ),
        compiler_params=pltpu.CompilerParams(vmem_limit_bytes=VMEM_BYTES),
    )(own, oth, cots, act)


def combine_kernel(back_ref, table_ref, out_ref):
    height, lanes = back_ref.shape[1:]
    toks = table_ref.shape[1]
    half = lanes // 2
    row = iota((lanes, 2 * toks), 0)
    col = iota((lanes, 2 * toks), 1)
    slot_row = row & (half - 1)
    fits = ((row >= half) == (col >= toks)) & (((col & (toks - 1)) >> 3) == (slot_row >> 2))
    wanted = jnp.where(fits, (slot_row & 3).astype(F32), 9.0)
    total = jnp.zeros((2 * height, 2 * toks), F32)
    for e in range(0, EXPERTS, 2):
        places = []
        for j in (e, e + 1):
            slot = table_ref[j : j + 1, :]
            slot = jnp.concatenate([slot, slot], axis=1)
            places.append(jnp.where(slot == wanted, 1.0, 0.0))
        place = jnp.concatenate(places, axis=0).astype(BF16)
        rows = [
            jnp.concatenate([back_ref[p * EXPERTS + e], back_ref[p * EXPERTS + e + 1]], axis=1)
            for p in range(PAIR)
        ]
        total = total + jnp.dot(
            jnp.concatenate(rows, axis=0), place, preferred_element_type=F32
        )
    total = total[:height] + total[height:]
    total = jnp.concatenate([total[:, :toks], total[:, toks:]], axis=0)
    pad = jnp.zeros((out_ref.shape[1] - 2 * height, toks), F32)
    out_ref[...] = jnp.transpose(jnp.concatenate([total, pad], axis=0)).astype(BF16)


def combine(back, table):
    return pl.pallas_call(
        combine_kernel,
        out_shape=jax.ShapeDtypeStruct((table.shape[1], 256), BF16),
        compiler_params=pltpu.CompilerParams(vmem_limit_bytes=VMEM_BYTES),
    )(back, table)


def sum_kernel(parts_ref, out_ref):
    total = parts_ref[0].astype(F32)
    for i in range(1, parts_ref.shape[0]):
        total = total + parts_ref[i].astype(F32)
    out_ref[...] = total[:, : out_ref.shape[1]].astype(BF16)


def add_parts(parts, width):
    return pl.pallas_call(
        sum_kernel, out_shape=jax.ShapeDtypeStruct((parts.shape[1], width), BF16)
    )(parts)


def exchange(value, axis):
    return lax.all_to_all(value, axis, split_axis=0, concat_axis=0, tiled=True)


SWAP = [(0, 1), (1, 0)]
WIDE = ("pair", "y", "x")


def shards(tokens, grad_out, routes, gate_probs, w_gate, w_up, w_down):
    tok_rows, width = tokens.shape
    dim = w_gate.shape[2]
    w_gate, w_up, w_down = w_gate[0], w_up[0], w_down[0]
    pair = lax.axis_index("pair").astype(jnp.int32).reshape(1)
    far = exchange(message(tokens, grad_out, routes, gate_probs), "far")
    slots, table = pack(pair, far.reshape(FAR * tok_rows, ROW), width)
    own = exchange(slots, WIDE).reshape(PAIR, dim, -1)
    oth = lax.ppermute(own, "core", SWAP)
    keep, send, cots, act = expert(own, oth, w_gate, w_up, w_down, width)
    back = (keep + lax.ppermute(send, "core", SWAP).astype(F32)).astype(BF16)
    back = exchange(back.reshape((PAIR * EXPERTS,) + back.shape[2:]), WIDE)
    part = combine(back, table)
    part = exchange(part.reshape(FAR, tok_rows, part.shape[1]), "far")
    grad_in = add_parts(part, width)
    grad_gate, grad_up, grad_down = weight_grads(own, oth, cots, act)
    return grad_in, grad_gate[None], grad_up[None], grad_down[None]


def solution(mesh):
    fine = Mesh(
        mesh.devices.reshape(FAR, PAIR, 2, 4, 4), ("far", "pair", "core", "y", "x")
    )
    dp, expert_axes = ("far", "pair", "core"), ("y", "x")
    in_specs = (
        P(dp, expert_axes),
        P(dp, expert_axes),
        P(dp, None),
        P(dp, None),
        P(expert_axes, dp, None),
        P(expert_axes, dp, None),
        P(expert_axes, dp, None),
    )
    out_specs = (
        P(dp, expert_axes),
        P(expert_axes, dp, None),
        P(expert_axes, dp, None),
        P(expert_axes, dp, None),
    )
    return jax.shard_map(shards, mesh=fine, in_specs=in_specs, out_specs=out_specs, check_vma=False)
```

```python
import jax
import jax.numpy as jnp
from jax import lax
from jax.experimental import pallas as pl
from jax.experimental.pallas import tpu as pltpu
from jax.sharding import Mesh, PartitionSpec as P

EXPERTS = 16
CAP = 4
TOP = 4
FAR = 16
PAIR = 2
BF16 = jnp.bfloat16
F32 = jnp.float32
VMEM_BYTES = 24 * 1024 * 1024
LAST = (((1,), (1,)), ((), ()))
FIRST = (((0,), (0,)), ((), ()))
GRAD_AT = 256
ROW = 512
STEP = 384


def iota(shape, dim):
    return lax.broadcasted_iota(jnp.int32, shape, dim)


def message_kernel(tokens_ref, grad_ref, routes_ref, probs_ref, out_ref):
    tok_rows, width = tokens_ref.shape
    eye = iota((tok_rows, tok_rows), 0) == iota((tok_rows, tok_rows), 1)

    def column(values):
        spread = jnp.broadcast_to(values, (tok_rows, tok_rows))
        return jnp.sum(jnp.where(eye, spread, 0.0), axis=1, keepdims=True)

    lane = iota((tok_rows, 128), 1)
    row = iota((tok_rows, 128), 0)
    expert_at = (lane & (EXPERTS - 1)).astype(F32)
    chosen = jnp.zeros((tok_rows, 128), F32)
    weight = jnp.zeros((tok_rows, 128), F32)
    for k in range(TOP):
        hit = expert_at == column(routes_ref[k : k + 1, :].astype(F32))
        chosen = jnp.where(hit, 1.0, chosen)
        weight = jnp.where(hit, column(probs_ref[k : k + 1, :]), weight)
    before = jnp.zeros((tok_rows, 128), F32)
    for s in range(1, tok_rows):
        before = before + jnp.where(row >= s, pltpu.roll(chosen, s, 0), 0.0)
    kind = lane >> 4
    meta = jnp.where(kind == 4, jnp.where(chosen > 0.0, before, -1.0), 0.0)
    rest = weight
    for part in range(3):
        piece = rest.astype(BF16).astype(F32)
        meta = jnp.where(kind == 5 + part, piece, meta)
        rest = rest - piece
    meta = meta.astype(BF16)
    blank = jnp.zeros((tok_rows, 128), BF16)
    for copy in range(out_ref.shape[0]):
        out_ref[copy, :, 128:256] = meta
        out_ref[copy, :, 0:width] = tokens_ref[...]
        out_ref[copy, :, GRAD_AT + 128 : ROW] = blank
        out_ref[copy, :, GRAD_AT : GRAD_AT + width] = grad_ref[...]


def message(tokens, grad_out, routes, probs):
    return pl.pallas_call(
        message_kernel,
        out_shape=jax.ShapeDtypeStruct((FAR, tokens.shape[0], ROW), BF16),
    )(tokens, grad_out, routes.T, probs.T)


def pack_kernel(pair_ref, msg_ref, out_ref, table_ref):
    toks = msg_ref.shape[0]
    width, lanes = out_ref.shape[1:]
    half = lanes // 2
    left = msg_ref[:, 0:GRAD_AT].astype(F32)
    left_t = jnp.transpose(left)
    right_t = jnp.transpose(msg_ref[:, GRAD_AT:ROW].astype(F32))
    table_ref[...] = left_t[width : width + EXPERTS]
    top = jnp.concatenate([left_t[:width], right_t[:width]], axis=1)
    parts = left_t[width + EXPERTS : width + 4 * EXPERTS]
    low = jnp.concatenate([jnp.zeros_like(parts), parts], axis=1)
    lhs = jnp.concatenate([top, low], axis=0).astype(BF16)
    pair = pair_ref[0]
    tok = iota((2 * toks, lanes), 0)
    lane = iota((2 * toks, lanes), 1)
    row = lane & (half - 1)
    is_in = (lane >= half) == (pair == 1)
    fits = (((tok & (toks - 1)) >> 3) == (row >> 2)) & ((tok < toks) == is_in)
    wanted = jnp.where(fits, (row & 3).astype(F32), 9.0)
    in_lane = (iota((1, lanes), 1) >= half) == (pair == 1)
    for e in range(0, EXPERTS, 2):
        places = []
        for j in (e, e + 1):
            slot = left[:, width + j : width + j + 1]
            slot = jnp.concatenate([slot, slot], axis=0)
            places.append(jnp.where(slot == wanted, 1.0, 0.0))
        place = jnp.concatenate(places, axis=1).astype(BF16)
        both = jnp.dot(lhs, place, preferred_element_type=F32)
        for j in (0, 1):
            block = both[:, j * lanes : (j + 1) * lanes]
            scale = block[width + e + j : width + e + j + 1]
            for part in (1, 2):
                at = width + part * EXPERTS + e + j
                scale = scale + block[at : at + 1]
            scale = jnp.where(in_lane, 1.0, scale)
            packed = (block[:width] * scale).astype(BF16)
            for p in range(PAIR):
                out_ref[p * EXPERTS + e + j] = packed


def pack(pair, msgs, width):
    toks = msgs.shape[0]
    return pl.pallas_call(
        pack_kernel,
        in_specs=[
            pl.BlockSpec(memory_space=pltpu.SMEM),
            pl.BlockSpec(memory_space=pltpu.VMEM),
        ],
        out_shape=(
            jax.ShapeDtypeStruct((PAIR * EXPERTS, width, toks), BF16),
            jax.ShapeDtypeStruct((EXPERTS, toks), F32),
        ),
        compiler_params=pltpu.CompilerParams(vmem_limit_bytes=VMEM_BYTES),
    )(pair, msgs)


def rows_at(own_ref, at):
    lanes = own_ref.shape[2]
    first = iota((at.size, lanes), 1) < lanes // 2
    even, odd = own_ref[0, at, :], own_ref[1, at, :]
    return jnp.where(first, even, odd), jnp.where(first, odd, even)


def turn(value):
    return pltpu.roll(value, value.shape[1] // 2, 1)


def expert_kernel(
    own_ref, wg_ref, wu_ref, wd_ref, hg_ref, hu_ref, hd_ref, back_ref, cots_ref, act_ref
):
    dim, lanes = own_ref.shape[1:]
    units = wg_ref.shape[0]
    width = back_ref.shape[1] * 2

    def both(at):
        return jnp.concatenate(
            [wg_ref[:, at], hg_ref[:, at], wu_ref[:, at], hu_ref[:, at]], axis=0
        )

    fwd = jnp.zeros((4 * units, lanes), F32)
    grad_act = jnp.zeros((2 * units, lanes), F32)
    for i in range(dim // STEP):
        at = pl.ds(i * STEP, STEP)
        rows_in, rows_grad = rows_at(own_ref, at)
        down = jnp.concatenate([wd_ref[:, at], hd_ref[:, at]], axis=0)
        fwd = fwd + jnp.dot(both(at), rows_in, preferred_element_type=F32)
        grad_act = grad_act + jnp.dot(down, rows_grad, preferred_element_type=F32)
    grad_act = turn(grad_act)
    pre_act, up_value = fwd[: 2 * units], fwd[2 * units :]
    sig = jax.nn.sigmoid(pre_act)
    silu = pre_act * sig
    slope = sig * (1.0 + pre_act * (1.0 - sig))
    act_ref[...] = turn(silu * up_value).astype(BF16)
    grad_pre = (grad_act * up_value * slope).astype(BF16)
    grad_upv = (grad_act * silu).astype(BF16)
    cots = jnp.concatenate([grad_pre, grad_upv], axis=0)
    cots_ref[...] = cots
    first = iota((width // 2, lanes), 1) < lanes // 2
    for i in range(dim // STEP):
        at = pl.ds(i * STEP, STEP)
        total = lax.dot_general(both(at), cots, FIRST, preferred_element_type=F32)
        for j in range(STEP // width):
            e = i * (STEP // width) + j
            upper = total[j * width : j * width + width // 2]
            lower = total[j * width + width // 2 : (j + 1) * width]
            back_ref[e] = jnp.where(first, upper, turn(lower)).astype(BF16)
            back_ref[EXPERTS + e] = jnp.where(first, turn(upper), lower).astype(BF16)


def expert(own, mine, other, width):
    units, dim = mine[0].shape
    lanes = own.shape[2]
    return pl.pallas_call(
        expert_kernel,
        out_shape=(
            jax.ShapeDtypeStruct((PAIR * EXPERTS, width // 2, lanes), BF16),
            jax.ShapeDtypeStruct((4 * units, lanes), BF16),
            jax.ShapeDtypeStruct((2 * units, lanes), BF16),
        ),
        cost_estimate=pl.CostEstimate(
            flops=2 * 10 * units * dim * lanes, bytes_accessed=6 << 20, transcendentals=0
        ),
        compiler_params=pltpu.CompilerParams(vmem_limit_bytes=VMEM_BYTES),
    )(own, *mine, *other)


def grads_kernel(own_ref, cots_ref, act_ref, gg_ref, gu_ref, gd_ref, send_ref):
    units, dim = gg_ref.shape
    for i in range(dim // STEP):
        at = pl.ds(i * STEP, STEP)
        rows_in, rows_grad = rows_at(own_ref, at)
        grads = lax.dot_general(cots_ref[...], rows_in, LAST, preferred_element_type=F32)
        down = lax.dot_general(act_ref[...], rows_grad, LAST, preferred_element_type=F32)
        gg_ref[:, at] = grads[:units]
        gu_ref[:, at] = grads[2 * units : 3 * units]
        gd_ref[:, at] = down[:units]
        send_ref[0, :, at] = grads[units : 2 * units].astype(BF16)
        send_ref[1, :, at] = grads[3 * units :].astype(BF16)
        send_ref[2, :, at] = down[units:].astype(BF16)


def weight_grads(own, cots, act):
    units, dim = act.shape[0] // 2, own.shape[1]
    grad = jax.ShapeDtypeStruct((units, dim), F32)
    return pl.pallas_call(
        grads_kernel,
        out_shape=(grad, grad, grad, jax.ShapeDtypeStruct((3, units, dim), BF16)),
        cost_estimate=pl.CostEstimate(
            flops=2 * 6 * units * dim * act.shape[1], bytes_accessed=7 << 20, transcendentals=0
        ),
        compiler_params=pltpu.CompilerParams(vmem_limit_bytes=VMEM_BYTES),
    )(own, cots, act)


def combine_kernel(back_ref, table_ref, out_ref):
    height, lanes = back_ref.shape[1:]
    toks = table_ref.shape[1]
    half = lanes // 2
    row = iota((lanes, 2 * toks), 0)
    col = iota((lanes, 2 * toks), 1)
    slot_row = row & (half - 1)
    fits = ((row >= half) == (col >= toks)) & (((col & (toks - 1)) >> 3) == (slot_row >> 2))
    wanted = jnp.where(fits, (slot_row & 3).astype(F32), 9.0)
    total = jnp.zeros((2 * height, 2 * toks), F32)
    for e in range(0, EXPERTS, 2):
        places = []
        for j in (e, e + 1):
            slot = table_ref[j : j + 1, :]
            slot = jnp.concatenate([slot, slot], axis=1)
            places.append(jnp.where(slot == wanted, 1.0, 0.0))
        place = jnp.concatenate(places, axis=0).astype(BF16)
        rows = [
            jnp.concatenate([back_ref[p * EXPERTS + e], back_ref[p * EXPERTS + e + 1]], axis=1)
            for p in range(PAIR)
        ]
        total = total + jnp.dot(
            jnp.concatenate(rows, axis=0), place, preferred_element_type=F32
        )
    total = total[:height] + total[height:]
    total = jnp.concatenate([total[:, :toks], total[:, toks:]], axis=0)
    pad = jnp.zeros((out_ref.shape[1] - 2 * height, toks), F32)
    out_ref[...] = jnp.transpose(jnp.concatenate([total, pad], axis=0)).astype(BF16)


def combine(back, table):
    return pl.pallas_call(
        combine_kernel,
        out_shape=jax.ShapeDtypeStruct((table.shape[1], 256), BF16),
        compiler_params=pltpu.CompilerParams(vmem_limit_bytes=VMEM_BYTES),
    )(back, table)


def exchange(value, axis, groups=None):
    return lax.all_to_all(
        value, axis, split_axis=0, concat_axis=0, tiled=True, axis_index_groups=groups
    )


SWAP = [(0, 1), (1, 0)]
WIDE = ("pair", "y", "x")


def along_z():
    return [[(FAR // 2 + i) % FAR * PAIR + p for i in range(FAR)] for p in range(PAIR)]


def shards(tokens, grad_out, routes, gate_probs, w_gate, w_up, w_down):
    tok_rows, width = tokens.shape
    dim = w_gate.shape[2]
    mine = (w_gate[0], w_up[0], w_down[0])
    other = tuple(lax.ppermute(w, "core", SWAP) for w in mine)
    pair = lax.axis_index("pair").astype(jnp.int32).reshape(1)
    far = exchange(message(tokens, grad_out, routes, gate_probs), ("far", "pair"), along_z())
    slots, table = pack(pair, far.reshape(FAR * tok_rows, ROW), width)
    own = exchange(slots, WIDE).reshape(PAIR, dim, -1)
    back, cots, act = expert(own, mine, other, width)
    part = combine(exchange(back, WIDE), table)
    part = exchange(part.reshape(FAR, tok_rows, part.shape[1]), ("far", "pair"), along_z())
    part = lax.optimization_barrier(part.astype(F32))
    grad_in = part.sum(axis=0)[:, :width].astype(BF16)
    *halves, send = weight_grads(own, cots, act)
    send = lax.ppermute(send, "core", SWAP)
    grads = [(half + send[i].astype(F32)).astype(BF16)[None] for i, half in enumerate(halves)]
    return grad_in, *grads


def solution(mesh):
    fine = Mesh(
        mesh.devices.reshape(FAR, PAIR, 2, 4, 4), ("far", "pair", "core", "y", "x")
    )
    dp, expert_axes = ("far", "pair", "core"), ("y", "x")
    in_specs = (
        P(dp, expert_axes),
        P(dp, expert_axes),
        P(dp, None),
        P(dp, None),
        P(expert_axes, dp, None),
        P(expert_axes, dp, None),
        P(expert_axes, dp, None),
    )
    out_specs = (
        P(dp, expert_axes),
        P(expert_axes, dp, None),
        P(expert_axes, dp, None),
        P(expert_axes, dp, None),
    )
    return jax.shard_map(shards, mesh=fine, in_specs=in_specs, out_specs=out_specs, check_vma=False)
```

```python
import jax
import jax.numpy as jnp
from jax import lax
from jax.experimental import pallas as pl
from jax.experimental.pallas import tpu as pltpu
from jax.sharding import Mesh, PartitionSpec as P

EXPERTS = 16
CAP = 4
TOP = 4
FAR = 16
PAIR = 2
BF16 = jnp.bfloat16
F32 = jnp.float32
VMEM_BYTES = 24 * 1024 * 1024
LAST = (((1,), (1,)), ((), ()))
FIRST = (((0,), (0,)), ((), ()))
STEP = 768


def iota(shape, dim):
    return lax.broadcasted_iota(jnp.int32, shape, dim)


def message_kernel(tokens_ref, grad_ref, routes_ref, probs_ref, out_ref):
    tok_rows, width = tokens_ref.shape
    eye = iota((tok_rows, tok_rows), 0) == iota((tok_rows, tok_rows), 1)

    def column(values):
        spread = jnp.broadcast_to(values, (tok_rows, tok_rows))
        return jnp.sum(jnp.where(eye, spread, 0.0), axis=1, keepdims=True)

    lane = iota((tok_rows, 128), 1)
    row = iota((tok_rows, 128), 0)
    expert_at = (lane & (EXPERTS - 1)).astype(F32)
    chosen = jnp.zeros((tok_rows, 128), F32)
    weight = jnp.zeros((tok_rows, 128), F32)
    for k in range(TOP):
        hit = expert_at == column(routes_ref[k : k + 1, :].astype(F32))
        chosen = jnp.where(hit, 1.0, chosen)
        weight = jnp.where(hit, column(probs_ref[k : k + 1, :]), weight)
    before = jnp.zeros((tok_rows, 128), F32)
    for s in range(1, tok_rows):
        before = before + jnp.where(row >= s, pltpu.roll(chosen, s, 0), 0.0)
    kind = lane >> 4
    meta = jnp.where(kind == 4, jnp.where(chosen > 0.0, before, -1.0), 0.0)
    rest = weight
    for part in range(3):
        piece = rest.astype(BF16).astype(F32)
        meta = jnp.where(kind == 5 + part, piece, meta)
        rest = rest - piece
    half = tok_rows // 2
    tokens, grad = tokens_ref[...].astype(F32), grad_ref[...].astype(F32)
    pad = jnp.zeros((tok_rows, 256 - width), F32)
    tokens = jnp.concatenate([tokens, pad], axis=1)
    grad = jnp.concatenate([grad, pad], axis=1)
    blocks = []
    for chunk in (tokens[:, :128], tokens[:, 128:] + meta, grad[:, :128]):
        blocks += [chunk[:half], chunk[half:]]
    blocks.append(grad[:half, 128:] + pltpu.roll(grad[:, 128:], 64, 1)[half:])
    blocks = [block.astype(BF16) for block in blocks]
    for copy in range(out_ref.shape[0]):
        for i, block in enumerate(blocks):
            out_ref[copy, i] = block


def message(tokens, grad_out, routes, probs):
    return pl.pallas_call(
        message_kernel,
        out_shape=jax.ShapeDtypeStruct((FAR, 7, tokens.shape[0] // 2, 128), BF16),
    )(tokens, grad_out, routes.T, probs.T)


def pack_kernel(pair_ref, msg_ref, out_ref, table_ref):
    toks = table_ref.shape[1]
    width, lanes = out_ref.shape[1:]
    half = lanes // 2

    def chunk(i):
        return msg_ref[:, 2 * i : 2 * i + 2].astype(F32).reshape(toks, 128)

    last = msg_ref[:, 6].astype(F32)
    last = jnp.stack([last, pltpu.roll(last, 64, 2)], axis=1).reshape(toks, 128)
    left = jnp.concatenate([chunk(0), chunk(1)], axis=1)
    left_t = jnp.transpose(left)
    right_t = jnp.transpose(jnp.concatenate([chunk(2), last], axis=1))
    table_ref[...] = left_t[width : width + EXPERTS]
    top = jnp.concatenate([left_t[:width], right_t[:width]], axis=1)
    parts = left_t[width + EXPERTS : width + 4 * EXPERTS]
    low = jnp.concatenate([jnp.zeros_like(parts), parts], axis=1)
    lhs = jnp.concatenate([top, low], axis=0).astype(BF16)
    pair = pair_ref[0]
    tok = iota((2 * toks, lanes), 0)
    lane = iota((2 * toks, lanes), 1)
    row = lane & (half - 1)
    is_in = (lane >= half) == (pair == 1)
    fits = (((tok & (toks - 1)) >> 3) == (row >> 2)) & ((tok < toks) == is_in)
    wanted = jnp.where(fits, (row & 3).astype(F32), 9.0)
    in_lane = (iota((1, lanes), 1) >= half) == (pair == 1)
    for e in range(0, EXPERTS, 2):
        places = []
        for j in (e, e + 1):
            slot = left[:, width + j : width + j + 1]
            slot = jnp.concatenate([slot, slot], axis=0)
            places.append(jnp.where(slot == wanted, 1.0, 0.0))
        place = jnp.concatenate(places, axis=1).astype(BF16)
        both = jnp.dot(lhs, place, preferred_element_type=F32)
        for j in (0, 1):
            block = both[:, j * lanes : (j + 1) * lanes]
            scale = block[width + e + j : width + e + j + 1]
            for part in (1, 2):
                at = width + part * EXPERTS + e + j
                scale = scale + block[at : at + 1]
            scale = jnp.where(in_lane, 1.0, scale)
            packed = (block[:width] * scale).astype(BF16)
            for p in range(PAIR):
                out_ref[p * EXPERTS + e + j] = packed


def pack(pair, msgs, width):
    toks = msgs.shape[0] * msgs.shape[2] * 2
    return pl.pallas_call(
        pack_kernel,
        in_specs=[
            pl.BlockSpec(memory_space=pltpu.SMEM),
            pl.BlockSpec(memory_space=pltpu.VMEM),
        ],
        out_shape=(
            jax.ShapeDtypeStruct((PAIR * EXPERTS, width, toks), BF16),
            jax.ShapeDtypeStruct((EXPERTS, toks), F32),
        ),
        compiler_params=pltpu.CompilerParams(vmem_limit_bytes=VMEM_BYTES),
    )(pair, msgs)


def rows_at(own_ref, at):
    lanes = own_ref.shape[2]
    first = iota((at.size, lanes), 1) < lanes // 2
    even, odd = own_ref[0, at, :], own_ref[1, at, :]
    return jnp.where(first, even, odd), jnp.where(first, odd, even)


def turn(value):
    return pltpu.roll(value, value.shape[1] // 2, 1)


def expert_kernel(
    own_ref, wg_ref, wu_ref, wd_ref, hg_ref, hu_ref, hd_ref, back_ref, cots_ref,
    total_ref, sems,
):
    dim, lanes = own_ref.shape[1:]
    units = wg_ref.shape[0]
    width = back_ref.shape[1] * 2

    def both(at):
        return jnp.concatenate(
            [wg_ref[:, at], hg_ref[:, at], wu_ref[:, at], hu_ref[:, at]], axis=0
        )

    fwd = jnp.zeros((4 * units, lanes), F32)
    grad_act = jnp.zeros((2 * units, lanes), F32)
    for i in range(dim // STEP):
        at = pl.ds(i * STEP, STEP)
        rows_in, rows_grad = rows_at(own_ref, at)
        down = jnp.concatenate([wd_ref[:, at], hd_ref[:, at]], axis=0)
        fwd = fwd + jnp.dot(both(at), rows_in, preferred_element_type=F32)
        grad_act = grad_act + jnp.dot(down, rows_grad, preferred_element_type=F32)
    grad_act = turn(grad_act)
    pre_act, up_value = fwd[: 2 * units], fwd[2 * units :]
    sig = jax.nn.sigmoid(pre_act)
    silu = pre_act * sig
    slope = sig * (1.0 + pre_act * (1.0 - sig))
    grad_pre = (grad_act * up_value * slope).astype(BF16)
    grad_upv = (grad_act * silu).astype(BF16)
    cots = jnp.concatenate([grad_pre, grad_upv], axis=0)
    cots_ref[: 4 * units] = cots
    cots_ref[4 * units :] = turn(silu * up_value).astype(BF16)
    wide = jnp.concatenate([cots, turn(cots)], axis=1)
    first = iota((width // 2, lanes), 1) < lanes // 2
    per = STEP // width
    stores = []
    for i in range(dim // STEP):
        at = pl.ds(i * STEP, STEP)
        total = lax.dot_general(both(at), wide, FIRST, preferred_element_type=F32)
        for j in range(per):
            e = i * per + j
            upper = total[j * width : j * width + width // 2]
            lower = total[j * width + width // 2 : (j + 1) * width]
            even = jnp.where(first, upper[:, :lanes], lower[:, lanes:])
            odd = jnp.where(first, upper[:, lanes:], lower[:, :lanes])
            total_ref[e] = even.astype(BF16)
            total_ref[EXPERTS + e] = odd.astype(BF16)
        for p in range(PAIR):
            part = pl.ds(p * EXPERTS + i * per, per)
            copy = pltpu.make_async_copy(total_ref.at[part], back_ref.at[part], sems.at[i, p])
            copy.start()
            stores.append(copy)
    for copy in stores:
        copy.wait()


def expert(own, mine, other, width):
    units, dim = mine[0].shape
    lanes = own.shape[2]
    back = (PAIR * EXPERTS, width // 2, lanes)
    return pl.pallas_call(
        expert_kernel,
        out_shape=(
            pltpu.HBM(back, BF16),
            jax.ShapeDtypeStruct((6 * units, lanes), BF16),
        ),
        out_specs=(
            pl.BlockSpec(memory_space=pltpu.HBM),
            pl.BlockSpec(memory_space=pltpu.VMEM),
        ),
        scratch_shapes=[
            pltpu.VMEM(back, BF16),
            pltpu.SemaphoreType.DMA((dim // STEP, PAIR)),
        ],
        cost_estimate=pl.CostEstimate(
            flops=2 * 10 * units * dim * lanes, bytes_accessed=6 << 20, transcendentals=0
        ),
        compiler_params=pltpu.CompilerParams(vmem_limit_bytes=VMEM_BYTES),
    )(own, *mine, *other)


def grads_kernel(
    own_ref, cots_ref, gg_ref, gu_ref, gd_ref, send_ref, half_ref, keep_ref, give_ref, sems
):
    units, dim = gg_ref.shape
    steps = dim // STEP
    load = pltpu.make_async_copy(cots_ref, half_ref, sems.at[steps, 0])
    load.start()
    load.wait()
    stores = []
    for i in range(steps):
        at = pl.ds(i * STEP, STEP)
        rows_in, rows_grad = rows_at(own_ref, at)
        grads = lax.dot_general(
            half_ref[: 4 * units], rows_in, LAST, preferred_element_type=F32
        )
        down = lax.dot_general(
            half_ref[4 * units :], rows_grad, LAST, preferred_element_type=F32
        )
        for j, (value, begin) in enumerate(((grads, 0), (grads, 2 * units), (down, 0))):
            keep_ref[j, :, at] = value[begin : begin + units]
            give_ref[j, :, at] = value[begin + units : begin + 2 * units].astype(BF16)
        for j, ref in enumerate((gg_ref, gu_ref, gd_ref)):
            stores.append(
                pltpu.make_async_copy(keep_ref.at[j, :, at], ref.at[:, at], sems.at[i, j])
            )
            stores[-1].start()
            stores.append(
                pltpu.make_async_copy(
                    give_ref.at[j, :, at], send_ref.at[j, :, at], sems.at[i, 3 + j]
                )
            )
            stores[-1].start()
    for copy in stores:
        copy.wait()


def weight_grads(own, cots):
    units, dim = cots.shape[0] // 6, own.shape[1]
    grad = pltpu.HBM((units, dim), F32)
    hbm = pl.BlockSpec(memory_space=pltpu.HBM)
    return pl.pallas_call(
        grads_kernel,
        in_specs=[pl.BlockSpec(memory_space=pltpu.VMEM), hbm],
        out_specs=(hbm, hbm, hbm, hbm),
        out_shape=(grad, grad, grad, pltpu.HBM((3, units, dim), BF16)),
        scratch_shapes=[
            pltpu.VMEM(cots.shape, BF16),
            pltpu.VMEM((3, units, dim), F32),
            pltpu.VMEM((3, units, dim), BF16),
            pltpu.SemaphoreType.DMA((dim // STEP + 1, 6)),
        ],
        cost_estimate=pl.CostEstimate(
            flops=2 * 6 * units * dim * cots.shape[1], bytes_accessed=7 << 20, transcendentals=0
        ),
        compiler_params=pltpu.CompilerParams(vmem_limit_bytes=VMEM_BYTES),
    )(own, cots)


def combine_kernel(back_ref, table_ref, out_ref):
    height, lanes = back_ref.shape[1:]
    toks = table_ref.shape[1]
    half = lanes // 2
    row = iota((lanes, 2 * toks), 0)
    col = iota((lanes, 2 * toks), 1)
    slot_row = row & (half - 1)
    fits = ((row >= half) == (col >= toks)) & (((col & (toks - 1)) >> 3) == (slot_row >> 2))
    wanted = jnp.where(fits, (slot_row & 3).astype(F32), 9.0)
    total = jnp.zeros((2 * height, 2 * toks), F32)
    for e in range(0, EXPERTS, 2):
        places = []
        for j in (e, e + 1):
            slot = table_ref[j : j + 1, :]
            slot = jnp.concatenate([slot, slot], axis=1)
            places.append(jnp.where(slot == wanted, 1.0, 0.0))
        place = jnp.concatenate(places, axis=0).astype(BF16)
        rows = [
            jnp.concatenate([back_ref[p * EXPERTS + e], back_ref[p * EXPERTS + e + 1]], axis=1)
            for p in range(PAIR)
        ]
        total = total + jnp.dot(
            jnp.concatenate(rows, axis=0), place, preferred_element_type=F32
        )
    total = total[:height] + total[height:]
    total = jnp.concatenate([total[:, :toks], total[:, toks:]], axis=0)
    pad = jnp.zeros((out_ref.shape[1] - 2 * height, toks), F32)
    out_ref[...] = jnp.transpose(jnp.concatenate([total, pad], axis=0)).astype(BF16)


def combine(back, table):
    return pl.pallas_call(
        combine_kernel,
        out_shape=jax.ShapeDtypeStruct((table.shape[1], 256), BF16),
        compiler_params=pltpu.CompilerParams(vmem_limit_bytes=VMEM_BYTES),
    )(back, table)


ALL = ("far", "pair", "core", "y", "x")


def wide_groups():
    planes = 2 * FAR * PAIR
    groups = []
    for first in range(0, planes, 4):
        for one, two in ((first, first + 2), (first + 3, (first + 5) % planes)):
            groups.append(
                [plane * EXPERTS + e for plane in (one, two) for e in range(EXPERTS)]
            )
    return groups


def exchange(value, axis, groups=None):
    return lax.all_to_all(
        value, axis, split_axis=0, concat_axis=0, tiled=True, axis_index_groups=groups
    )


SWAP = [(0, 1), (1, 0)]


def along_z():
    return [[(FAR // 2 + i) % FAR * PAIR + p for i in range(FAR)] for p in range(PAIR)]


def shards(tokens, grad_out, routes, gate_probs, w_gate, w_up, w_down):
    tok_rows, width = tokens.shape
    dim = w_gate.shape[2]
    mine = (w_gate[0], w_up[0], w_down[0])
    msg = message(tokens, grad_out, routes, gate_probs)
    msg, *early = lax.optimization_barrier((msg, *mine))
    other = [lax.ppermute(w, "core", SWAP) for w in early]
    pair = (lax.axis_index("pair") + lax.axis_index("core")).astype(jnp.int32).reshape(1) % PAIR
    far = exchange(msg, ("far", "pair"), along_z())
    far, *other = lax.optimization_barrier((far, *other))
    slots, table = pack(pair, far, width)
    own = exchange(slots, ALL, wide_groups()).reshape(PAIR, dim, -1)
    back, cots = expert(own, mine, other, width)
    part = combine(exchange(back, ALL, wide_groups()), table)
    part = exchange(part.reshape(FAR, tok_rows, part.shape[1]), ("far", "pair"), along_z())
    part = lax.optimization_barrier(part.astype(F32))
    grad_in = part.sum(axis=0)[:, :width].astype(BF16)
    *halves, send = weight_grads(own, cots)
    send = lax.ppermute(send, "core", SWAP)
    grads = [(half + send[i].astype(F32)).astype(BF16)[None] for i, half in enumerate(halves)]
    return grad_in, *grads


def solution(mesh):
    fine = Mesh(
        mesh.devices.reshape(FAR, PAIR, 2, 4, 4), ("far", "pair", "core", "y", "x")
    )
    dp, expert_axes = ("far", "pair", "core"), ("y", "x")
    in_specs = (
        P(dp, expert_axes),
        P(dp, expert_axes),
        P(dp, None),
        P(dp, None),
        P(expert_axes, dp, None),
        P(expert_axes, dp, None),
        P(expert_axes, dp, None),
    )
    out_specs = (
        P(dp, expert_axes),
        P(expert_axes, dp, None),
        P(expert_axes, dp, None),
        P(expert_axes, dp, None),
    )
    return jax.shard_map(shards, mesh=fine, in_specs=in_specs, out_specs=out_specs, check_vma=False)
```

```python
import jax
import jax.numpy as jnp
from jax import lax
from jax.experimental import pallas as pl
from jax.experimental.pallas import tpu as pltpu
from jax.sharding import Mesh, PartitionSpec as P

EXPERTS = 16
CAP = 4
TOP = 4
FAR = 16
PAIR = 2
BF16 = jnp.bfloat16
F32 = jnp.float32
VMEM_BYTES = 12 * 1024 * 1024
LAST = (((1,), (1,)), ((), ()))
FIRST = (((0,), (0,)), ((), ()))
STEP = 384
GATHER_FROM = 10
SUM_FROM = 8


def iota(shape, dim):
    return lax.broadcasted_iota(jnp.int32, shape, dim)


def message_kernel(tokens_ref, grad_ref, routes_ref, probs_ref, out_ref):
    tok_rows, width = tokens_ref.shape
    eye = iota((tok_rows, tok_rows), 0) == iota((tok_rows, tok_rows), 1)

    def column(values):
        spread = jnp.broadcast_to(values, (tok_rows, tok_rows))
        return jnp.sum(jnp.where(eye, spread, 0.0), axis=1, keepdims=True)

    lane = iota((tok_rows, 128), 1)
    row = iota((tok_rows, 128), 0)
    expert_at = (lane & (EXPERTS - 1)).astype(F32)
    chosen = jnp.zeros((tok_rows, 128), F32)
    weight = jnp.zeros((tok_rows, 128), F32)
    for k in range(TOP):
        hit = expert_at == column(routes_ref[k : k + 1, :].astype(F32))
        chosen = jnp.where(hit, 1.0, chosen)
        weight = jnp.where(hit, column(probs_ref[k : k + 1, :]), weight)
    before = jnp.zeros((tok_rows, 128), F32)
    for s in range(1, tok_rows):
        before = before + jnp.where(row >= s, pltpu.roll(chosen, s, 0), 0.0)
    kind = lane >> 4
    meta = jnp.where(kind == 4, jnp.where(chosen > 0.0, before, -1.0), 0.0)
    rest = weight
    for part in range(3):
        piece = rest.astype(BF16).astype(F32)
        meta = jnp.where(kind == 5 + part, piece, meta)
        rest = rest - piece
    half = tok_rows // 2
    tokens, grad = tokens_ref[...].astype(F32), grad_ref[...].astype(F32)
    pad = jnp.zeros((tok_rows, 256 - width), F32)
    tokens = jnp.concatenate([tokens, pad], axis=1)
    grad = jnp.concatenate([grad, pad], axis=1)
    blocks = []
    for chunk in (tokens[:, :128], tokens[:, 128:] + meta, grad[:, :128]):
        blocks += [chunk[:half], chunk[half:]]
    blocks.append(grad[:half, 128:] + pltpu.roll(grad[:, 128:], 64, 1)[half:])
    blocks = [block.astype(BF16) for block in blocks]
    for copy in range(out_ref.shape[0]):
        for i, block in enumerate(blocks):
            out_ref[copy, i] = block


def message(tokens, grad_out, routes, probs):
    return pl.pallas_call(
        message_kernel,
        out_shape=pltpu.VMEM((FAR, 7, tokens.shape[0] // 2, 128), BF16),
    )(tokens, grad_out, routes.T, probs.T)


def pack_kernel(pair_ref, msg_ref, out_ref, table_ref):
    toks = table_ref.shape[1]
    width, lanes = out_ref.shape[1:]
    half = lanes // 2

    def chunk(i):
        return msg_ref[:, 2 * i : 2 * i + 2].astype(F32).reshape(toks, 128)

    last = msg_ref[:, 6].astype(F32)
    last = jnp.stack([last, pltpu.roll(last, 64, 2)], axis=1).reshape(toks, 128)
    left = jnp.concatenate([chunk(0), chunk(1)], axis=1)
    left_t = jnp.transpose(left)
    right_t = jnp.transpose(jnp.concatenate([chunk(2), last], axis=1))
    table_ref[...] = left_t[width : width + EXPERTS]
    top = jnp.concatenate([left_t[:width], right_t[:width]], axis=1)
    parts = left_t[width + EXPERTS : width + 4 * EXPERTS]
    low = jnp.concatenate([jnp.zeros_like(parts), parts], axis=1)
    lhs = jnp.concatenate([top, low], axis=0).astype(BF16)
    pair = pair_ref[0]
    tok = iota((2 * toks, lanes), 0)
    lane = iota((2 * toks, lanes), 1)
    row = lane & (half - 1)
    is_in = (lane >= half) == (pair == 1)
    fits = (((tok & (toks - 1)) >> 3) == (row >> 2)) & ((tok < toks) == is_in)
    wanted = jnp.where(fits, (row & 3).astype(F32), 9.0)
    in_lane = (iota((1, lanes), 1) >= half) == (pair == 1)
    for e in range(0, EXPERTS, 2):
        places = []
        for j in (e, e + 1):
            slot = left[:, width + j : width + j + 1]
            slot = jnp.concatenate([slot, slot], axis=0)
            places.append(jnp.where(slot == wanted, 1.0, 0.0))
        place = jnp.concatenate(places, axis=1).astype(BF16)
        both = jnp.dot(lhs, place, preferred_element_type=F32)
        for j in (0, 1):
            block = both[:, j * lanes : (j + 1) * lanes]
            scale = block[width + e + j : width + e + j + 1]
            for part in (1, 2):
                at = width + part * EXPERTS + e + j
                scale = scale + block[at : at + 1]
            scale = jnp.where(in_lane, 1.0, scale)
            packed = (block[:width] * scale).astype(BF16)
            for p in range(PAIR):
                out_ref[p * EXPERTS + e + j] = packed


def pack(pair, msgs, width):
    toks = msgs.shape[0] * msgs.shape[2] * 2
    return pl.pallas_call(
        pack_kernel,
        in_specs=[
            pl.BlockSpec(memory_space=pltpu.SMEM),
            pl.BlockSpec(memory_space=pltpu.VMEM),
        ],
        out_shape=(
            jax.ShapeDtypeStruct((PAIR * EXPERTS, width, toks), BF16),
            jax.ShapeDtypeStruct((EXPERTS, toks), F32),
        ),
        compiler_params=pltpu.CompilerParams(vmem_limit_bytes=VMEM_BYTES),
    )(pair, msgs)


def rows_at(own_ref, at):
    lanes = own_ref.shape[2]
    first = iota((at.size, lanes), 1) < lanes // 2
    even, odd = own_ref[0, at, :], own_ref[1, at, :]
    return jnp.where(first, even, odd), jnp.where(first, odd, even)


def turn(value):
    return pltpu.roll(value, value.shape[1] // 2, 1)


def expert_kernel(
    own_ref, wg_ref, wu_ref, wd_ref, hg_ref, hu_ref, hd_ref, back_ref, cots_ref,
    down_ref, sems,
):
    dim, lanes = own_ref.shape[1:]
    units = wg_ref.shape[0]
    width = back_ref.shape[1] * 2
    loads = []
    for i in range(units // 48):
        part = pl.ds(48 * i, 48)
        loads.append(pltpu.make_async_copy(hd_ref.at[part], down_ref.at[part], sems.at[i]))
        loads[-1].start()

    def both(at):
        return jnp.concatenate(
            [wg_ref[:, at], hg_ref[:, at], wu_ref[:, at], hu_ref[:, at]], axis=0
        )

    fwd = jnp.zeros((4 * units, lanes), F32)
    for i in range(dim // STEP):
        at = pl.ds(i * STEP, STEP)
        fwd = fwd + jnp.dot(both(at), rows_at(own_ref, at)[0], preferred_element_type=F32)
    for copy in loads:
        copy.wait()
    grad_act = jnp.zeros((2 * units, lanes), F32)
    for i in range(dim // STEP):
        at = pl.ds(i * STEP, STEP)
        down = jnp.concatenate([wd_ref[:, at], down_ref[:, at]], axis=0)
        grad_act = grad_act + jnp.dot(down, rows_at(own_ref, at)[1], preferred_element_type=F32)
    grad_act = turn(grad_act)
    pre_act, up_value = fwd[: 2 * units], fwd[2 * units :]
    sig = jax.nn.sigmoid(pre_act)
    silu = pre_act * sig
    slope = sig * (1.0 + pre_act * (1.0 - sig))
    grad_pre = (grad_act * up_value * slope).astype(BF16)
    grad_upv = (grad_act * silu).astype(BF16)
    cots = jnp.concatenate([grad_pre, grad_upv], axis=0)
    activation = turn(silu * up_value).astype(BF16)
    for half in (0, 1):
        at = half * units
        cots_ref[half, :units] = grad_pre[at : at + units]
        cots_ref[half, units : 2 * units] = grad_upv[at : at + units]
        cots_ref[half, 2 * units :] = activation[at : at + units]
    wide = jnp.concatenate([cots, turn(cots)], axis=1)
    first = iota((width // 2, lanes), 1) < lanes // 2
    per = STEP // width
    for i in range(dim // STEP):
        at = pl.ds(i * STEP, STEP)
        total = lax.dot_general(both(at), wide, FIRST, preferred_element_type=F32)
        for j in range(per):
            e = i * per + j
            upper = total[j * width : j * width + width // 2]
            lower = total[j * width + width // 2 : (j + 1) * width]
            even = jnp.where(first, upper[:, :lanes], lower[:, lanes:])
            odd = jnp.where(first, upper[:, lanes:], lower[:, :lanes])
            back_ref[e] = even.astype(BF16)
            back_ref[EXPERTS + e] = odd.astype(BF16)


def expert(own, mine, other, width):
    units, dim = mine[0].shape
    lanes = own.shape[2]
    back = (PAIR * EXPERTS, width // 2, lanes)
    vmem = pl.BlockSpec(memory_space=pltpu.VMEM)
    return pl.pallas_call(
        expert_kernel,
        in_specs=[vmem] * 6 + [pl.BlockSpec(memory_space=pl.ANY)],
        scratch_shapes=[
            pltpu.VMEM((units, dim), BF16),
            pltpu.SemaphoreType.DMA((units // 48,)),
        ],
        out_shape=(
            pltpu.VMEM(back, BF16),
            jax.ShapeDtypeStruct((2, 3 * units, lanes), BF16),
        ),
        cost_estimate=pl.CostEstimate(
            flops=2 * 10 * units * dim * lanes, bytes_accessed=6 << 20, transcendentals=0
        ),
        compiler_params=pltpu.CompilerParams(vmem_limit_bytes=VMEM_BYTES),
    )(own, *mine, *other)


def unit_grads(own_ref, cots_ref, half, at):
    units = cots_ref.shape[1] // 3
    rows_in, rows_grad = rows_at(own_ref, at)
    up = lax.dot_general(
        cots_ref[half, : 2 * units], rows_in, LAST, preferred_element_type=F32
    )
    down = lax.dot_general(
        cots_ref[half, 2 * units :], rows_grad, LAST, preferred_element_type=F32
    )
    return up[:units], up[units:], down


def give_kernel(own_ref, cots_ref, send_ref, held_ref, sems):
    stores = []
    for i in range(own_ref.shape[1] // STEP):
        at = pl.ds(i * STEP, STEP)
        for j, value in enumerate(unit_grads(own_ref, cots_ref, 1, at)):
            held_ref[j, :, at] = value.astype(BF16)
        copy = pltpu.make_async_copy(held_ref.at[:, :, at], send_ref.at[:, :, at], sems.at[i])
        copy.start()
        stores.append(copy)
    for copy in stores:
        copy.wait()


def keep_kernel(own_ref, cots_ref, recv_ref, gg_ref, gu_ref, gd_ref, held_ref, sems):
    stores = []
    for i in range(own_ref.shape[1] // STEP):
        at = pl.ds(i * STEP, STEP)
        for j, value in enumerate(unit_grads(own_ref, cots_ref, 0, at)):
            held_ref[j, :, at] = (value + recv_ref[j, :, at].astype(F32)).astype(BF16)
        for j, ref in enumerate((gg_ref, gu_ref, gd_ref)):
            copy = pltpu.make_async_copy(held_ref.at[j, :, at], ref.at[:, at], sems.at[i, j])
            copy.start()
            stores.append(copy)
    for copy in stores:
        copy.wait()


def weight_grads(own, cots):
    units, dim = cots.shape[1] // 3, own.shape[1]
    steps, all_grads = dim // STEP, (3, units, dim)
    grad = pltpu.HBM((units, dim), BF16)
    hbm = pl.BlockSpec(memory_space=pltpu.HBM)
    params = dict(
        cost_estimate=pl.CostEstimate(
            flops=2 * 3 * units * dim * cots.shape[2], bytes_accessed=4 << 20, transcendentals=0
        ),
        compiler_params=pltpu.CompilerParams(vmem_limit_bytes=VMEM_BYTES),
    )
    send = pl.pallas_call(
        give_kernel,
        out_specs=hbm,
        out_shape=pltpu.HBM(all_grads, BF16),
        scratch_shapes=[pltpu.VMEM(all_grads, BF16), pltpu.SemaphoreType.DMA((steps,))],
        **params,
    )(own, cots)
    recv = lax.ppermute(send, "core", SWAP)
    return pl.pallas_call(
        keep_kernel,
        out_specs=(hbm, hbm, hbm),
        out_shape=(grad, grad, grad),
        scratch_shapes=[pltpu.VMEM(all_grads, BF16), pltpu.SemaphoreType.DMA((steps, 3))],
        **params,
    )(own, cots, recv)


def combine_kernel(back_ref, table_ref, out_ref):
    height, lanes = back_ref.shape[1:]
    toks = table_ref.shape[1]
    half = lanes // 2
    row = iota((lanes, 2 * toks), 0)
    col = iota((lanes, 2 * toks), 1)
    slot_row = row & (half - 1)
    fits = ((row >= half) == (col >= toks)) & (((col & (toks - 1)) >> 3) == (slot_row >> 2))
    wanted = jnp.where(fits, (slot_row & 3).astype(F32), 9.0)
    total = jnp.zeros((2 * height, 2 * toks), F32)
    for e in range(0, EXPERTS, 2):
        places = []
        for j in (e, e + 1):
            slot = table_ref[j : j + 1, :]
            slot = jnp.concatenate([slot, slot], axis=1)
            places.append(jnp.where(slot == wanted, 1.0, 0.0))
        place = jnp.concatenate(places, axis=0).astype(BF16)
        rows = [
            jnp.concatenate([back_ref[p * EXPERTS + e], back_ref[p * EXPERTS + e + 1]], axis=1)
            for p in range(PAIR)
        ]
        total = total + jnp.dot(
            jnp.concatenate(rows, axis=0), place, preferred_element_type=F32
        )
    total = total[:height] + total[height:]
    total = jnp.concatenate([total[:, :toks], total[:, toks:]], axis=0)
    pad = jnp.zeros((out_ref.shape[1] - 2 * height, toks), F32)
    total = jnp.transpose(jnp.concatenate([total, pad], axis=0)).astype(BF16)
    ahead = (GATHER_FROM - SUM_FROM) % FAR * (toks // FAR)
    out_ref[ahead:] = total[: toks - ahead]
    out_ref[:ahead] = total[toks - ahead :]


def combine(back, table):
    return pl.pallas_call(
        combine_kernel,
        out_shape=pltpu.VMEM((table.shape[1], 256), BF16),
        compiler_params=pltpu.CompilerParams(vmem_limit_bytes=VMEM_BYTES),
    )(back, table)


ALL = ("far", "pair", "core", "y", "x")


def wide_groups():
    planes = 2 * FAR * PAIR
    groups = []
    for first in range(0, planes, 4):
        for one, two in ((first, first + 2), (first + 3, (first + 5) % planes)):
            groups.append(
                [plane * EXPERTS + e for plane in (one, two) for e in range(EXPERTS)]
            )
    return groups


def exchange(value, axis, groups=None):
    return lax.all_to_all(
        value, axis, split_axis=0, concat_axis=0, tiled=True, axis_index_groups=groups
    )


SWAP = [(0, 1), (1, 0)]


def along_z(first):
    return [[(first + i) % FAR * PAIR + p for i in range(FAR)] for p in range(PAIR)]


def shards(tokens, grad_out, routes, gate_probs, w_gate, w_up, w_down):
    tok_rows, width = tokens.shape
    dim = w_gate.shape[2]
    mine = (w_gate[0], w_up[0], w_down[0])
    msg = message(tokens, grad_out, routes, gate_probs)
    msg, *early = lax.optimization_barrier((msg, *mine))
    other = [lax.ppermute(w, "core", SWAP) for w in early]
    pair = (lax.axis_index("pair") + lax.axis_index("core")).astype(jnp.int32).reshape(1) % PAIR
    far = exchange(msg, ("far", "pair"), along_z(GATHER_FROM))
    far, *other = lax.optimization_barrier((far, *other))
    slots, table = pack(pair, far, width)
    own = exchange(slots, ALL, wide_groups()).reshape(PAIR, dim, -1)
    back, cots = expert(own, mine, other, width)
    grads = weight_grads(own, cots)
    back, *grads = lax.optimization_barrier((exchange(back, ALL, wide_groups()), *grads))
    part = combine(back, table)
    part = exchange(part.reshape(FAR, tok_rows, part.shape[1]), ("far", "pair"), along_z(SUM_FROM))
    part = lax.optimization_barrier(part.astype(F32))
    grad_in = part.sum(axis=0)[:, :width].astype(BF16)
    return grad_in, *(grad[None] for grad in grads)


def solution(mesh):
    fine = Mesh(
        mesh.devices.reshape(FAR, PAIR, 2, 4, 4), ("far", "pair", "core", "y", "x")
    )
    dp, expert_axes = ("far", "pair", "core"), ("y", "x")
    in_specs = (
        P(dp, expert_axes),
        P(dp, expert_axes),
        P(dp, None),
        P(dp, None),
        P(expert_axes, dp, None),
        P(expert_axes, dp, None),
        P(expert_axes, dp, None),
    )
    out_specs = (
        P(dp, expert_axes),
        P(expert_axes, dp, None),
        P(expert_axes, dp, None),
        P(expert_axes, dp, None),
    )
    return jax.shard_map(shards, mesh=fine, in_specs=in_specs, out_specs=out_specs, check_vma=False)
```

```python
import jax
import jax.numpy as jnp
from jax import lax
from jax.experimental import pallas as pl
from jax.experimental.pallas import tpu as pltpu
from jax.sharding import Mesh, PartitionSpec as P

EXPERTS = 16
CAP = 4
TOP = 4
FAR = 16
PAIR = 2
BF16 = jnp.bfloat16
F32 = jnp.float32
VMEM_BYTES = 12 * 1024 * 1024
LAST = (((1,), (1,)), ((), ()))
FIRST = (((0,), (0,)), ((), ()))
STEP = 384
GATHER_FROM = 10
SUM_FROM = 8


def iota(shape, dim):
    return lax.broadcasted_iota(jnp.int32, shape, dim)


def message_kernel(tokens_ref, grad_ref, routes_ref, probs_ref, out_ref):
    tok_rows, width = tokens_ref.shape
    eye = iota((tok_rows, tok_rows), 0) == iota((tok_rows, tok_rows), 1)

    def column(values):
        spread = jnp.broadcast_to(values, (tok_rows, tok_rows))
        return jnp.sum(jnp.where(eye, spread, 0.0), axis=1, keepdims=True)

    lane = iota((tok_rows, 128), 1)
    row = iota((tok_rows, 128), 0)
    expert_at = (lane & (EXPERTS - 1)).astype(F32)
    chosen = jnp.zeros((tok_rows, 128), F32)
    weight = jnp.zeros((tok_rows, 128), F32)
    for k in range(TOP):
        hit = expert_at == column(routes_ref[k : k + 1, :].astype(F32))
        chosen = jnp.where(hit, 1.0, chosen)
        weight = jnp.where(hit, column(probs_ref[k : k + 1, :]), weight)
    before = jnp.zeros((tok_rows, 128), F32)
    for s in range(1, tok_rows):
        before = before + jnp.where(row >= s, pltpu.roll(chosen, s, 0), 0.0)
    kind = lane >> 4
    meta = jnp.where(kind == 4, jnp.where(chosen > 0.0, before, -1.0), 0.0)
    rest = weight
    for part in range(3):
        piece = rest.astype(BF16).astype(F32)
        meta = jnp.where(kind == 5 + part, piece, meta)
        rest = rest - piece
    half = tok_rows // 2
    tokens, grad = tokens_ref[...].astype(F32), grad_ref[...].astype(F32)
    pad = jnp.zeros((tok_rows, 256 - width), F32)
    tokens = jnp.concatenate([tokens, pad], axis=1)
    grad = jnp.concatenate([grad, pad], axis=1)
    blocks = []
    for chunk in (tokens[:, :128], tokens[:, 128:] + meta, grad[:, :128]):
        blocks += [chunk[:half], chunk[half:]]
    blocks.append(grad[:half, 128:] + pltpu.roll(grad[:, 128:], 64, 1)[half:])
    blocks = [block.astype(BF16) for block in blocks]
    for copy in range(out_ref.shape[0]):
        for i, block in enumerate(blocks):
            out_ref[copy, i] = block


def message(tokens, grad_out, routes, probs):
    return pl.pallas_call(
        message_kernel,
        out_shape=pltpu.VMEM((FAR, 7, tokens.shape[0] // 2, 128), BF16),
    )(tokens, grad_out, routes.T, probs.T)


def pack_kernel(pair_ref, msg_ref, out_ref, table_ref):
    toks = table_ref.shape[1]
    width, lanes = out_ref.shape[1:]
    half = lanes // 2

    def chunk(i):
        return msg_ref[:, 2 * i : 2 * i + 2].astype(F32).reshape(toks, 128)

    last = msg_ref[:, 6].astype(F32)
    last = jnp.stack([last, pltpu.roll(last, 64, 2)], axis=1).reshape(toks, 128)
    left = jnp.concatenate([chunk(0), chunk(1)], axis=1)
    left_t = jnp.transpose(left)
    right_t = jnp.transpose(jnp.concatenate([chunk(2), last], axis=1))
    table_ref[...] = left_t[width : width + EXPERTS]
    top = jnp.concatenate([left_t[:width], right_t[:width]], axis=1)
    parts = left_t[width + EXPERTS : width + 4 * EXPERTS]
    low = jnp.concatenate([jnp.zeros_like(parts), parts], axis=1)
    lhs = jnp.concatenate([top, low], axis=0).astype(BF16)
    pair = pair_ref[0]
    tok = iota((2 * toks, lanes), 0)
    lane = iota((2 * toks, lanes), 1)
    row = lane & (half - 1)
    is_in = (lane >= half) == (pair == 1)
    fits = (((tok & (toks - 1)) >> 3) == (row >> 2)) & ((tok < toks) == is_in)
    wanted = jnp.where(fits, (row & 3).astype(F32), 9.0)
    in_lane = (iota((1, lanes), 1) >= half) == (pair == 1)
    for e in range(0, EXPERTS, 2):
        places = []
        for j in (e, e + 1):
            slot = left[:, width + j : width + j + 1]
            slot = jnp.concatenate([slot, slot], axis=0)
            places.append(jnp.where(slot == wanted, 1.0, 0.0))
        place = jnp.concatenate(places, axis=1).astype(BF16)
        both = jnp.dot(lhs, place, preferred_element_type=F32)
        for j in (0, 1):
            block = both[:, j * lanes : (j + 1) * lanes]
            scale = block[width + e + j : width + e + j + 1]
            for part in (1, 2):
                at = width + part * EXPERTS + e + j
                scale = scale + block[at : at + 1]
            scale = jnp.where(in_lane, 1.0, scale)
            packed = (block[:width] * scale).astype(BF16)
            for p in range(PAIR):
                out_ref[p * EXPERTS + e + j] = packed


def pack(pair, msgs, width):
    toks = msgs.shape[0] * msgs.shape[2] * 2
    return pl.pallas_call(
        pack_kernel,
        in_specs=[
            pl.BlockSpec(memory_space=pltpu.SMEM),
            pl.BlockSpec(memory_space=pltpu.VMEM),
        ],
        out_shape=(
            jax.ShapeDtypeStruct((PAIR * EXPERTS, width, toks), BF16),
            jax.ShapeDtypeStruct((EXPERTS, toks), F32),
        ),
        compiler_params=pltpu.CompilerParams(vmem_limit_bytes=VMEM_BYTES),
    )(pair, msgs)


def rows_at(own_ref, at):
    lanes = own_ref.shape[2]
    first = iota((at.size, lanes), 1) < lanes // 2
    even, odd = own_ref[0, at, :], own_ref[1, at, :]
    return jnp.where(first, even, odd), jnp.where(first, odd, even)


def turn(value):
    return pltpu.roll(value, value.shape[1] // 2, 1)


def expert_kernel(
    own_ref, wg_ref, wu_ref, wd_ref, hg_ref, hu_ref, hd_ref, back_ref, cots_ref,
    down_ref, sems,
):
    dim, lanes = own_ref.shape[1:]
    units = wg_ref.shape[0]
    width = back_ref.shape[1] * 2
    loads = []
    for i in range(units // 96):
        part = pl.ds(96 * i, 96)
        loads.append(pltpu.make_async_copy(hd_ref.at[part], down_ref.at[part], sems.at[i]))
        loads[-1].start()

    def both(at):
        return jnp.concatenate(
            [wg_ref[:, at], hg_ref[:, at], wu_ref[:, at], hu_ref[:, at]], axis=0
        )

    fwd = jnp.zeros((4 * units, lanes), F32)
    for i in range(dim // STEP):
        at = pl.ds(i * STEP, STEP)
        fwd = fwd + jnp.dot(both(at), rows_at(own_ref, at)[0], preferred_element_type=F32)
    for copy in loads:
        copy.wait()
    grad_act = jnp.zeros((2 * units, lanes), F32)
    for i in range(dim // STEP):
        at = pl.ds(i * STEP, STEP)
        down = jnp.concatenate([wd_ref[:, at], down_ref[:, at]], axis=0)
        grad_act = grad_act + jnp.dot(down, rows_at(own_ref, at)[1], preferred_element_type=F32)
    grad_act = turn(grad_act)
    pre_act, up_value = fwd[: 2 * units], fwd[2 * units :]
    sig = jax.nn.sigmoid(pre_act)
    silu = pre_act * sig
    slope = sig * (1.0 + pre_act * (1.0 - sig))
    grad_pre = (grad_act * up_value * slope).astype(BF16)
    grad_upv = (grad_act * silu).astype(BF16)
    cots = jnp.concatenate([grad_pre, grad_upv], axis=0)
    activation = turn(silu * up_value).astype(BF16)
    for half in (0, 1):
        at = half * units
        cots_ref[half, :units] = grad_pre[at : at + units]
        cots_ref[half, units : 2 * units] = grad_upv[at : at + units]
        cots_ref[half, 2 * units :] = activation[at : at + units]
    wide = jnp.concatenate([cots, turn(cots)], axis=1)
    first = iota((width // 2, lanes), 1) < lanes // 2
    per = STEP // width
    for i in range(dim // STEP):
        at = pl.ds(i * STEP, STEP)
        total = lax.dot_general(both(at), wide, FIRST, preferred_element_type=F32)
        for j in range(per):
            e = i * per + j
            upper = total[j * width : j * width + width // 2]
            lower = total[j * width + width // 2 : (j + 1) * width]
            even = jnp.where(first, upper[:, :lanes], lower[:, lanes:])
            odd = jnp.where(first, upper[:, lanes:], lower[:, :lanes])
            back_ref[e] = even.astype(BF16)
            back_ref[EXPERTS + e] = odd.astype(BF16)


def expert(own, mine, other, width):
    units, dim = mine[0].shape
    lanes = own.shape[2]
    back = (PAIR * EXPERTS, width // 2, lanes)
    vmem = pl.BlockSpec(memory_space=pltpu.VMEM)
    return pl.pallas_call(
        expert_kernel,
        in_specs=[vmem] * 6 + [pl.BlockSpec(memory_space=pl.ANY)],
        scratch_shapes=[
            pltpu.VMEM((units, dim), BF16),
            pltpu.SemaphoreType.DMA((units // 96,)),
        ],
        out_shape=(
            pltpu.VMEM(back, BF16),
            jax.ShapeDtypeStruct((2, 3 * units, lanes), BF16),
        ),
        cost_estimate=pl.CostEstimate(
            flops=2 * 10 * units * dim * lanes, bytes_accessed=6 << 20, transcendentals=0
        ),
        compiler_params=pltpu.CompilerParams(vmem_limit_bytes=VMEM_BYTES),
    )(own, *mine, *other)


def unit_grads(own_ref, cots_ref, half, at):
    units = cots_ref.shape[1] // 3
    rows_in, rows_grad = rows_at(own_ref, at)
    up = lax.dot_general(
        cots_ref[half, : 2 * units], rows_in, LAST, preferred_element_type=F32
    )
    down = lax.dot_general(
        cots_ref[half, 2 * units :], rows_grad, LAST, preferred_element_type=F32
    )
    return up[:units], up[units:], down


def give_kernel(own_ref, cots_ref, send_ref, held_ref, sems):
    stores = []
    for i in range(own_ref.shape[1] // STEP):
        at = pl.ds(i * STEP, STEP)
        for j, value in enumerate(unit_grads(own_ref, cots_ref, 1, at)):
            held_ref[j, :, at] = value.astype(BF16)
        copy = pltpu.make_async_copy(held_ref.at[:, :, at], send_ref.at[:, :, at], sems.at[i])
        copy.start()
        stores.append(copy)
    for copy in stores:
        copy.wait()


def keep_kernel(own_ref, cots_ref, recv_ref, gg_ref, gu_ref, gd_ref, held_ref, sems):
    stores = []
    for i in range(own_ref.shape[1] // STEP):
        at = pl.ds(i * STEP, STEP)
        for j, value in enumerate(unit_grads(own_ref, cots_ref, 0, at)):
            held_ref[j, :, at] = (value + recv_ref[j, :, at].astype(F32)).astype(BF16)
        for j, ref in enumerate((gg_ref, gu_ref, gd_ref)):
            copy = pltpu.make_async_copy(held_ref.at[j, :, at], ref.at[:, at], sems.at[i, j])
            copy.start()
            stores.append(copy)
    for copy in stores:
        copy.wait()


def weight_grads(own, cots):
    units, dim = cots.shape[1] // 3, own.shape[1]
    steps, all_grads = dim // STEP, (3, units, dim)
    grad = pltpu.HBM((units, dim), BF16)
    hbm = pl.BlockSpec(memory_space=pltpu.HBM)
    params = dict(
        cost_estimate=pl.CostEstimate(
            flops=2 * 3 * units * dim * cots.shape[2], bytes_accessed=4 << 20, transcendentals=0
        ),
        compiler_params=pltpu.CompilerParams(vmem_limit_bytes=VMEM_BYTES),
    )
    send = pl.pallas_call(
        give_kernel,
        out_specs=hbm,
        out_shape=pltpu.HBM(all_grads, BF16),
        scratch_shapes=[pltpu.VMEM(all_grads, BF16), pltpu.SemaphoreType.DMA((steps,))],
        **params,
    )(own, cots)
    recv = lax.ppermute(send, "core", SWAP)
    return pl.pallas_call(
        keep_kernel,
        out_specs=(hbm, hbm, hbm),
        out_shape=(grad, grad, grad),
        scratch_shapes=[pltpu.VMEM(all_grads, BF16), pltpu.SemaphoreType.DMA((steps, 3))],
        **params,
    )(own, cots, recv)


def combine_kernel(back_ref, table_ref, out_ref):
    height, lanes = back_ref.shape[1:]
    toks = table_ref.shape[1]
    half = lanes // 2
    row = iota((lanes, 2 * toks), 0)
    col = iota((lanes, 2 * toks), 1)
    slot_row = row & (half - 1)
    fits = ((row >= half) == (col >= toks)) & (((col & (toks - 1)) >> 3) == (slot_row >> 2))
    wanted = jnp.where(fits, (slot_row & 3).astype(F32), 9.0)
    total = jnp.zeros((2 * height, 2 * toks), F32)
    for e in range(0, EXPERTS, 2):
        places = []
        for j in (e, e + 1):
            slot = table_ref[j : j + 1, :]
            slot = jnp.concatenate([slot, slot], axis=1)
            places.append(jnp.where(slot == wanted, 1.0, 0.0))
        place = jnp.concatenate(places, axis=0).astype(BF16)
        rows = [
            jnp.concatenate([back_ref[p * EXPERTS + e], back_ref[p * EXPERTS + e + 1]], axis=1)
            for p in range(PAIR)
        ]
        total = total + jnp.dot(
            jnp.concatenate(rows, axis=0), place, preferred_element_type=F32
        )
    total = total[:height] + total[height:]
    total = jnp.concatenate([total[:, :toks], total[:, toks:]], axis=0)
    pad = jnp.zeros((out_ref.shape[1] - 2 * height, toks), F32)
    total = jnp.transpose(jnp.concatenate([total, pad], axis=0)).astype(BF16)
    ahead = (GATHER_FROM - SUM_FROM) % FAR * (toks // FAR)
    out_ref[ahead:] = total[: toks - ahead]
    out_ref[:ahead] = total[toks - ahead :]


def combine(back, table):
    return pl.pallas_call(
        combine_kernel,
        out_shape=pltpu.VMEM((table.shape[1], 256), BF16),
        compiler_params=pltpu.CompilerParams(vmem_limit_bytes=VMEM_BYTES),
    )(back, table)


ALL = ("far", "pair", "core", "y", "x")


def wide_groups():
    planes = 2 * FAR * PAIR
    groups = []
    for first in range(0, planes, 4):
        for one, two in ((first, first + 2), (first + 1, first + 3)):
            groups.append(
                [plane * EXPERTS + e for plane in (one, two) for e in range(EXPERTS)]
            )
    return groups


def exchange(value, axis, groups=None):
    return lax.all_to_all(
        value, axis, split_axis=0, concat_axis=0, tiled=True, axis_index_groups=groups
    )


SWAP = [(0, 1), (1, 0)]


def along_z(first):
    return [[(first + i) % FAR * PAIR + p for i in range(FAR)] for p in range(PAIR)]


def shards(tokens, grad_out, routes, gate_probs, w_gate, w_up, w_down):
    tok_rows, width = tokens.shape
    dim = w_gate.shape[2]
    mine = (w_gate[0], w_up[0], w_down[0])
    msg = message(tokens, grad_out, routes, gate_probs)
    msg, *early = lax.optimization_barrier((msg, *mine))
    other = [lax.ppermute(w, "core", SWAP) for w in early]
    pair = lax.axis_index("pair").astype(jnp.int32).reshape(1)
    far = exchange(msg, ("far", "pair"), along_z(GATHER_FROM))
    far, *other = lax.optimization_barrier((far, *other))
    slots, table = pack(pair, far, width)
    own = exchange(slots, ALL, wide_groups()).reshape(PAIR, dim, -1)
    back, cots = expert(own, mine, other, width)
    grads = weight_grads(own, cots)
    back, *grads = lax.optimization_barrier((exchange(back, ALL, wide_groups()), *grads))
    part = combine(back, table)
    part = exchange(part.reshape(FAR, tok_rows, part.shape[1]), ("far", "pair"), along_z(SUM_FROM))
    part = lax.optimization_barrier(part.astype(F32))
    grad_in = part.sum(axis=0)[:, :width].astype(BF16)
    return grad_in, *(grad[None] for grad in grads)


def solution(mesh):
    fine = Mesh(
        mesh.devices.reshape(FAR, PAIR, 2, 4, 4), ("far", "pair", "core", "y", "x")
    )
    dp, expert_axes = ("far", "pair", "core"), ("y", "x")
    in_specs = (
        P(dp, expert_axes),
        P(dp, expert_axes),
        P(dp, None),
        P(dp, None),
        P(expert_axes, dp, None),
        P(expert_axes, dp, None),
        P(expert_axes, dp, None),
    )
    out_specs = (
        P(dp, expert_axes),
        P(expert_axes, dp, None),
        P(expert_axes, dp, None),
        P(expert_axes, dp, None),
    )
    return jax.shard_map(shards, mesh=fine, in_specs=in_specs, out_specs=out_specs, check_vma=False)
```

```python
import jax
import jax.numpy as jnp
from jax import lax
from jax.experimental import pallas as pl
from jax.experimental.pallas import tpu as pltpu
from jax.sharding import Mesh, PartitionSpec as P

EXPERTS = 16
CAP = 4
TOP = 4
FAR = 16
PAIR = 2
BF16 = jnp.bfloat16
F32 = jnp.float32
VMEM_BYTES = 12 * 1024 * 1024
LAST = (((1,), (1,)), ((), ()))
FIRST = (((0,), (0,)), ((), ()))
STEP = 384
GATHER_FROM = 10
SUM_FROM = 8


def iota(shape, dim):
    return lax.broadcasted_iota(jnp.int32, shape, dim)


def message_kernel(tokens_ref, grad_ref, routes_ref, probs_ref, out_ref):
    tok_rows, width = tokens_ref.shape
    eye = iota((tok_rows, tok_rows), 0) == iota((tok_rows, tok_rows), 1)

    def column(values):
        spread = jnp.broadcast_to(values, (tok_rows, tok_rows))
        return jnp.sum(jnp.where(eye, spread, 0.0), axis=1, keepdims=True)

    lane = iota((tok_rows, 128), 1)
    row = iota((tok_rows, 128), 0)
    expert_at = (lane & (EXPERTS - 1)).astype(F32)
    chosen = jnp.zeros((tok_rows, 128), F32)
    weight = jnp.zeros((tok_rows, 128), F32)
    for k in range(TOP):
        hit = expert_at == column(routes_ref[k : k + 1, :].astype(F32))
        chosen = jnp.where(hit, 1.0, chosen)
        weight = jnp.where(hit, column(probs_ref[k : k + 1, :]), weight)
    before = jnp.zeros((tok_rows, 128), F32)
    for s in range(1, tok_rows):
        before = before + jnp.where(row >= s, pltpu.roll(chosen, s, 0), 0.0)
    kind = lane >> 4
    meta = jnp.where(kind == 4, jnp.where(chosen > 0.0, before, -1.0), 0.0)
    rest = weight
    for part in range(3):
        piece = rest.astype(BF16).astype(F32)
        meta = jnp.where(kind == 5 + part, piece, meta)
        rest = rest - piece
    half = tok_rows // 2
    tokens, grad = tokens_ref[...].astype(F32), grad_ref[...].astype(F32)
    pad = jnp.zeros((tok_rows, 256 - width), F32)
    tokens = jnp.concatenate([tokens, pad], axis=1)
    grad = jnp.concatenate([grad, pad], axis=1)
    blocks = []
    for chunk in (tokens[:, :128], tokens[:, 128:] + meta, grad[:, :128]):
        blocks += [chunk[:half], chunk[half:]]
    blocks.append(grad[:half, 128:] + pltpu.roll(grad[:, 128:], 64, 1)[half:])
    blocks = [block.astype(BF16) for block in blocks]
    for copy in range(out_ref.shape[0]):
        for i, block in enumerate(blocks):
            out_ref[copy, i] = block


def message(tokens, grad_out, routes, probs):
    return pl.pallas_call(
        message_kernel,
        out_shape=pltpu.VMEM((FAR, 7, tokens.shape[0] // 2, 128), BF16),
    )(tokens, grad_out, routes.T, probs.T)


def pack_kernel(pair_ref, msg_ref, out_ref, table_ref):
    toks = table_ref.shape[1]
    width, lanes = out_ref.shape[1:]
    half = lanes // 2

    def chunk(i):
        return msg_ref[:, 2 * i : 2 * i + 2].astype(F32).reshape(toks, 128)

    last = msg_ref[:, 6].astype(F32)
    last = jnp.stack([last, pltpu.roll(last, 64, 2)], axis=1).reshape(toks, 128)
    left = jnp.concatenate([chunk(0), chunk(1)], axis=1)
    left_t = jnp.transpose(left)
    right_t = jnp.transpose(jnp.concatenate([chunk(2), last], axis=1))
    table_ref[...] = left_t[width : width + EXPERTS]
    top = jnp.concatenate([left_t[:width], right_t[:width]], axis=1)
    parts = left_t[width + EXPERTS : width + 4 * EXPERTS]
    low = jnp.concatenate([jnp.zeros_like(parts), parts], axis=1)
    lhs = jnp.concatenate([top, low], axis=0).astype(BF16)
    pair = pair_ref[0]
    tok = iota((2 * toks, lanes), 0)
    lane = iota((2 * toks, lanes), 1)
    row = lane & (half - 1)
    is_in = (lane >= half) == (pair == 1)
    fits = (((tok & (toks - 1)) >> 3) == (row >> 2)) & ((tok < toks) == is_in)
    wanted = jnp.where(fits, (row & 3).astype(F32), 9.0)
    in_lane = (iota((1, lanes), 1) >= half) == (pair == 1)
    for e in range(0, EXPERTS, 2):
        places = []
        for j in (e, e + 1):
            slot = left[:, width + j : width + j + 1]
            slot = jnp.concatenate([slot, slot], axis=0)
            places.append(jnp.where(slot == wanted, 1.0, 0.0))
        place = jnp.concatenate(places, axis=1).astype(BF16)
        both = jnp.dot(lhs, place, preferred_element_type=F32)
        for j in (0, 1):
            block = both[:, j * lanes : (j + 1) * lanes]
            scale = block[width + e + j : width + e + j + 1]
            for part in (1, 2):
                at = width + part * EXPERTS + e + j
                scale = scale + block[at : at + 1]
            scale = jnp.where(in_lane, 1.0, scale)
            packed = (block[:width] * scale).astype(BF16)
            for p in range(PAIR):
                out_ref[p * EXPERTS + e + j] = packed


def pack(pair, msgs, width):
    toks = msgs.shape[0] * msgs.shape[2] * 2
    return pl.pallas_call(
        pack_kernel,
        in_specs=[
            pl.BlockSpec(memory_space=pltpu.SMEM),
            pl.BlockSpec(memory_space=pltpu.VMEM),
        ],
        out_shape=(
            jax.ShapeDtypeStruct((PAIR * EXPERTS, width, toks), BF16),
            jax.ShapeDtypeStruct((EXPERTS, toks), F32),
        ),
        compiler_params=pltpu.CompilerParams(vmem_limit_bytes=VMEM_BYTES),
    )(pair, msgs)


def rows_at(own_ref, at):
    lanes = own_ref.shape[2]
    first = iota((at.size, lanes), 1) < lanes // 2
    even, odd = own_ref[0, at, :], own_ref[1, at, :]
    return jnp.where(first, even, odd), jnp.where(first, odd, even)


def turn(value):
    return pltpu.roll(value, value.shape[1] // 2, 1)


def expert_kernel(
    own_ref, wg_ref, wu_ref, wd_ref, hg_ref, hu_ref, hd_ref, back_ref, cots_ref,
    down_ref, sems,
):
    dim, lanes = own_ref.shape[1:]
    units = wg_ref.shape[0]
    width = back_ref.shape[1] * 2
    loads = []
    for i in range(units // 96):
        part = pl.ds(96 * i, 96)
        loads.append(pltpu.make_async_copy(hd_ref.at[part], down_ref.at[part], sems.at[i]))
        loads[-1].start()

    def both(at):
        return jnp.concatenate(
            [wg_ref[:, at], hg_ref[:, at], wu_ref[:, at], hu_ref[:, at]], axis=0
        )

    fwd = jnp.zeros((4 * units, lanes), F32)
    for i in range(dim // STEP):
        at = pl.ds(i * STEP, STEP)
        fwd = fwd + jnp.dot(both(at), rows_at(own_ref, at)[0], preferred_element_type=F32)
    for copy in loads:
        copy.wait()
    grad_act = jnp.zeros((2 * units, lanes), F32)
    for i in range(dim // STEP):
        at = pl.ds(i * STEP, STEP)
        down = jnp.concatenate([wd_ref[:, at], down_ref[:, at]], axis=0)
        grad_act = grad_act + jnp.dot(down, rows_at(own_ref, at)[1], preferred_element_type=F32)
    grad_act = turn(grad_act)
    pre_act, up_value = fwd[: 2 * units], fwd[2 * units :]
    sig = jax.nn.sigmoid(pre_act)
    silu = pre_act * sig
    slope = sig * (1.0 + pre_act * (1.0 - sig))
    grad_pre = (grad_act * up_value * slope).astype(BF16)
    grad_upv = (grad_act * silu).astype(BF16)
    cots = jnp.concatenate([grad_pre, grad_upv], axis=0)
    activation = turn(silu * up_value).astype(BF16)
    for half in (0, 1):
        at = half * units
        cots_ref[half, :units] = grad_pre[at : at + units]
        cots_ref[half, units : 2 * units] = grad_upv[at : at + units]
        cots_ref[half, 2 * units :] = activation[at : at + units]
    wide = jnp.concatenate([cots, turn(cots)], axis=1)
    first = iota((width // 2, lanes), 1) < lanes // 2
    per = STEP // width
    for i in range(dim // STEP):
        at = pl.ds(i * STEP, STEP)
        total = lax.dot_general(both(at), wide, FIRST, preferred_element_type=F32)
        for j in range(per):
            e = i * per + j
            upper = total[j * width : j * width + width // 2]
            lower = total[j * width + width // 2 : (j + 1) * width]
            even = jnp.where(first, upper[:, :lanes], lower[:, lanes:])
            odd = jnp.where(first, upper[:, lanes:], lower[:, :lanes])
            back_ref[e] = even.astype(BF16)
            back_ref[EXPERTS + e] = odd.astype(BF16)


def expert(own, mine, other, width):
    units, dim = mine[0].shape
    lanes = own.shape[2]
    back = (PAIR * EXPERTS, width // 2, lanes)
    vmem = pl.BlockSpec(memory_space=pltpu.VMEM)
    return pl.pallas_call(
        expert_kernel,
        in_specs=[vmem] * 6 + [pl.BlockSpec(memory_space=pl.ANY)],
        scratch_shapes=[
            pltpu.VMEM((units, dim), BF16),
            pltpu.SemaphoreType.DMA((units // 96,)),
        ],
        out_shape=(
            pltpu.VMEM(back, BF16),
            jax.ShapeDtypeStruct((2, 3 * units, lanes), BF16),
        ),
        cost_estimate=pl.CostEstimate(
            flops=2 * 10 * units * dim * lanes, bytes_accessed=6 << 20, transcendentals=0
        ),
        compiler_params=pltpu.CompilerParams(vmem_limit_bytes=VMEM_BYTES),
    )(own, *mine, *other)


def unit_grads(own_ref, cots_ref, half, at):
    units = cots_ref.shape[1] // 3
    rows_in, rows_grad = rows_at(own_ref, at)
    up = lax.dot_general(
        cots_ref[half, : 2 * units], rows_in, LAST, preferred_element_type=F32
    )
    down = lax.dot_general(
        cots_ref[half, 2 * units :], rows_grad, LAST, preferred_element_type=F32
    )
    return up[:units], up[units:], down


def give_kernel(own_ref, cots_ref, send_ref, held_ref, sems):
    stores = []
    for i in range(own_ref.shape[1] // STEP):
        at = pl.ds(i * STEP, STEP)
        for j, value in enumerate(unit_grads(own_ref, cots_ref, 1, at)):
            held_ref[j, :, at] = value.astype(BF16)
        copy = pltpu.make_async_copy(held_ref.at[:, :, at], send_ref.at[:, :, at], sems.at[i])
        copy.start()
        stores.append(copy)
    for copy in stores:
        copy.wait()


def keep_kernel(own_ref, cots_ref, recv_ref, gg_ref, gu_ref, gd_ref, held_ref, sems):
    stores = []
    for i in range(own_ref.shape[1] // STEP):
        at = pl.ds(i * STEP, STEP)
        for j, value in enumerate(unit_grads(own_ref, cots_ref, 0, at)):
            held_ref[j, :, at] = (value + recv_ref[j, :, at].astype(F32)).astype(BF16)
        for j, ref in enumerate((gg_ref, gu_ref, gd_ref)):
            copy = pltpu.make_async_copy(held_ref.at[j, :, at], ref.at[:, at], sems.at[i, j])
            copy.start()
            stores.append(copy)
    for copy in stores:
        copy.wait()


def weight_grads(own, cots):
    units, dim = cots.shape[1] // 3, own.shape[1]
    steps, all_grads = dim // STEP, (3, units, dim)
    grad = pltpu.HBM((units, dim), BF16)
    hbm = pl.BlockSpec(memory_space=pltpu.HBM)
    params = dict(
        cost_estimate=pl.CostEstimate(
            flops=2 * 3 * units * dim * cots.shape[2], bytes_accessed=4 << 20, transcendentals=0
        ),
        compiler_params=pltpu.CompilerParams(vmem_limit_bytes=VMEM_BYTES),
    )
    send = pl.pallas_call(
        give_kernel,
        out_specs=hbm,
        out_shape=pltpu.HBM(all_grads, BF16),
        scratch_shapes=[pltpu.VMEM(all_grads, BF16), pltpu.SemaphoreType.DMA((steps,))],
        **params,
    )(own, cots)
    recv = lax.ppermute(send, "core", SWAP)
    return pl.pallas_call(
        keep_kernel,
        out_specs=(hbm, hbm, hbm),
        out_shape=(grad, grad, grad),
        scratch_shapes=[pltpu.VMEM(all_grads, BF16), pltpu.SemaphoreType.DMA((steps, 3))],
        **params,
    )(own, cots, recv)


def combine_kernel(back_ref, table_ref, out_ref):
    height, lanes = back_ref.shape[1:]
    toks = table_ref.shape[1]
    half = lanes // 2
    row = iota((lanes, 2 * toks), 0)
    col = iota((lanes, 2 * toks), 1)
    slot_row = row & (half - 1)
    fits = ((row >= half) == (col >= toks)) & (((col & (toks - 1)) >> 3) == (slot_row >> 2))
    wanted = jnp.where(fits, (slot_row & 3).astype(F32), 9.0)
    total = jnp.zeros((2 * height, 2 * toks), F32)
    for e in range(0, EXPERTS, 2):
        places = []
        for j in (e, e + 1):
            slot = table_ref[j : j + 1, :]
            slot = jnp.concatenate([slot, slot], axis=1)
            places.append(jnp.where(slot == wanted, 1.0, 0.0))
        place = jnp.concatenate(places, axis=0).astype(BF16)
        rows = [
            jnp.concatenate([back_ref[p * EXPERTS + e], back_ref[p * EXPERTS + e + 1]], axis=1)
            for p in range(PAIR)
        ]
        total = total + jnp.dot(
            jnp.concatenate(rows, axis=0), place, preferred_element_type=F32
        )
    total = total[:height] + total[height:]
    total = jnp.concatenate([total[:, :toks], total[:, toks:]], axis=0)
    pad = jnp.zeros((256 - 2 * height, toks), F32)
    total = jnp.transpose(jnp.concatenate([total, pad], axis=0))
    ahead = (GATHER_FROM - SUM_FROM) % FAR * (toks // FAR)
    total = jnp.concatenate([total[toks - ahead :], total[: toks - ahead]], axis=0)
    shape = (FAR, 2, toks // FAR // 2, 128)
    low = total[:, 128:].reshape(shape)
    out_ref[:, 0:2] = total[:, :128].reshape(shape).astype(BF16)
    out_ref[:, 2] = (low[:, 0] + pltpu.roll(low[:, 1], 64, 2)).astype(BF16)


def combine(back, table):
    return pl.pallas_call(
        combine_kernel,
        out_shape=pltpu.VMEM((FAR, 3, table.shape[1] // FAR // 2, 128), BF16),
        compiler_params=pltpu.CompilerParams(vmem_limit_bytes=VMEM_BYTES),
    )(back, table)


def sum_kernel(parts_ref, out_ref):
    total = parts_ref[0].astype(F32)
    for i in range(1, parts_ref.shape[0]):
        total = total + parts_ref[i].astype(F32)
    low = jnp.concatenate([total[2], pltpu.roll(total[2], 64, 1)], axis=0)
    out_ref[:, :128] = jnp.concatenate([total[0], total[1]], axis=0).astype(BF16)
    out_ref[:, 128:] = low[:, : out_ref.shape[1] - 128].astype(BF16)


def add_parts(parts, tok_rows, width):
    return pl.pallas_call(
        sum_kernel, out_shape=jax.ShapeDtypeStruct((tok_rows, width), BF16)
    )(parts)


ALL = ("far", "pair", "core", "y", "x")


def wide_groups():
    planes = 2 * FAR * PAIR
    groups = []
    for first in range(0, planes, 4):
        for one, two in ((first, first + 2), (first + 1, first + 3)):
            groups.append(
                [plane * EXPERTS + e for plane in (one, two) for e in range(EXPERTS)]
            )
    return groups


def exchange(value, axis, groups=None):
    return lax.all_to_all(
        value, axis, split_axis=0, concat_axis=0, tiled=True, axis_index_groups=groups
    )


SWAP = [(0, 1), (1, 0)]


def along_z(first):
    return [[(first + i) % FAR * PAIR + p for i in range(FAR)] for p in range(PAIR)]


def shards(tokens, grad_out, routes, gate_probs, w_gate, w_up, w_down):
    tok_rows, width = tokens.shape
    dim = w_gate.shape[2]
    mine = (w_gate[0], w_up[0], w_down[0])
    msg = message(tokens, grad_out, routes, gate_probs)
    msg, *early = lax.optimization_barrier((msg, *mine))
    other = [lax.ppermute(w, "core", SWAP) for w in early]
    pair = lax.axis_index("pair").astype(jnp.int32).reshape(1)
    far = exchange(msg, ("far", "pair"), along_z(GATHER_FROM))
    far, *other = lax.optimization_barrier((far, *other))
    slots, table = pack(pair, far, width)
    own = exchange(slots, ALL, wide_groups()).reshape(PAIR, dim, -1)
    back, cots = expert(own, mine, other, width)
    grads = weight_grads(own, cots)
    back, *grads = lax.optimization_barrier((exchange(back, ALL, wide_groups()), *grads))
    part = combine(back, table)
    part = exchange(part, ("far", "pair"), along_z(SUM_FROM))
    grad_in = add_parts(part, tok_rows, width)
    return grad_in, *(grad[None] for grad in grads)


def solution(mesh):
    fine = Mesh(
        mesh.devices.reshape(FAR, PAIR, 2, 4, 4), ("far", "pair", "core", "y", "x")
    )
    dp, expert_axes = ("far", "pair", "core"), ("y", "x")
    in_specs = (
        P(dp, expert_axes),
        P(dp, expert_axes),
        P(dp, None),
        P(dp, None),
        P(expert_axes, dp, None),
        P(expert_axes, dp, None),
        P(expert_axes, dp, None),
    )
    out_specs = (
        P(dp, expert_axes),
        P(expert_axes, dp, None),
        P(expert_axes, dp, None),
        P(expert_axes, dp, None),
    )
    return jax.shard_map(shards, mesh=fine, in_specs=in_specs, out_specs=out_specs, check_vma=False)
```
